32 devices in a mesh: seq: 8 (over z, core), mp: 4 (over y, x).
Axes of the slice: x: 2, y: 2, z: 4, core: 2. Of those that a mesh axis runs over, the one named last changes fastest.
Arguments:
- fine_rows: bfloat16 [24576, 4096], P(('seq', 'mp')), may hold values from -6 to 6
- w_inputs: bfloat16 [4096, 4, 4096], P(None, None, 'mp'), may hold values from -0.375 to 0.375
- w_out: bfloat16 [4096, 4096], P('mp'), may hold values from -0.09375 to 0.09375
- head_gain: float32 [4096], P('mp'), may hold values from 0.1 to 1.9
- decay_log: float32 [32, 6144], P('mp', 'seq'), may hold values from -1 to 0, as said below
Outputs:
- fine_output: bfloat16 [24576, 4096], P(('seq', 'mp'))
The draws below stay inside these ranges and needn't reach their ends.
Inputs may be any that keep to these rules, and one draw needn't show every extreme that they name: `decay_log`: entries are logarithms of decay factors, one for each head and coarse row.
All inputs are finite; a program needn't handle non-finite values.
Results may differ from the reference program's by a relative error of at most 0.018.
Values may be sent and summed in bfloat16 or wider, within the bound.
No kernel may reach another device: no remote copies, remote signals or barrier semaphores. Data moves between devices by JAX's collectives and lax.ppermute only.
A program may use at most 192 MiB of HBM per device.

```python
import math
import jax
import jax.numpy as jnp
from jax import lax

D = 4096
ATTENDER_NUMBER = 32
SF = 4
CH = 128
LC_DEV = 768
HEADS_DEV = 8
POOLED_SPAN = 6144
LF = 24576
N_MP = 4


def draw_decay_log(key, part):
    fast_share = 0.5
    kind_draw = jax.random.uniform(jax.random.fold_in(key, 1), (ATTENDER_NUMBER, 1))
    fast_rate = 1.0 / jnp.exp(jax.random.uniform(jax.random.fold_in(key, 2), (ATTENDER_NUMBER, 1), minval=math.log(30.0), maxval=math.log(50.0)))
    slow_rate = jnp.exp(jax.random.uniform(jax.random.fold_in(key, 3), (ATTENDER_NUMBER, 1), minval=math.log(0.3), maxval=math.log(0.8))) / POOLED_SPAN
    reference_speed = jnp.where(kind_draw < fast_share, fast_rate, slow_rate)
    shard_count = POOLED_SPAN // LC_DEV
    portion_scaling_factor = jnp.exp(jax.random.uniform(jax.random.fold_in(key, 4), (ATTENDER_NUMBER, shard_count, 1), minval=math.log(0.6), maxval=math.log(1.6)))
    portion_scaling_factor = jnp.broadcast_to(portion_scaling_factor, (ATTENDER_NUMBER, shard_count, LC_DEV)).reshape(ATTENDER_NUMBER, POOLED_SPAN)
    entry_scaling_factor = jax.random.uniform(jax.random.fold_in(key, 5), (ATTENDER_NUMBER, POOLED_SPAN), minval=0.5, maxval=1.5)
    spell_chosen = jax.random.uniform(jax.random.fold_in(key, 6), (ATTENDER_NUMBER, POOLED_SPAN))
    spell_extent = jnp.log(jax.random.uniform(jax.random.fold_in(key, 7), (ATTENDER_NUMBER, POOLED_SPAN), minval=0.5, maxval=0.8))
    spell_sequence_items = jnp.where(spell_chosen < 2.0 / POOLED_SPAN, spell_extent, 0.0)
    return (-reference_speed * portion_scaling_factor * entry_scaling_factor + spell_sequence_items).astype(jnp.float32)


def block_levels(own_key, extent, pieces, least, high):
    factor_of, own = 1.0, jax.random.fold_in(own_key, 6)
    for axis_at, shards_of in pieces:
        steps = jnp.exp(jax.random.uniform(jax.random.fold_in(own, axis_at), (shards_of,), jnp.float32, least / len(pieces), high / len(pieces)))
        factor_of = factor_of * jnp.repeat(steps, extent[axis_at] // shards_of).reshape([-1 if axis == axis_at else 1 for axis in range(len(extent))])
    return factor_of


def scatter_about(stream_key, extent, width, limit, cuts=(), held_as=jnp.bfloat16):
    array = width * jax.random.normal(stream_key, extent, jnp.float32)
    if cuts:
        array = array * block_levels(stream_key, extent, cuts, -0.22, 0.18)
    return jnp.clip(array, -limit, limit).astype(held_as)


def setup_inputs(seed: int = 0) -> dict:
    arg_keys = jax.random.split(jax.random.key(seed), 6)
    return {
        "fine_rows": scatter_about(arg_keys[0], (LF, D), 1.0, 6.0, ((0, 32),)),
        "w_inputs": scatter_about(arg_keys[1], (D, 4, D), (D // 16) ** -0.5, 0.375, ((2, 4),)),
        "w_out": scatter_about(arg_keys[2], (D, D), D ** -0.5, 0.09375, ((0, 4),)),
        "head_gain": jnp.clip(1.0 + 0.18 * jax.random.normal(arg_keys[3], (D,), jnp.float32), 0.1, 1.9),
        "decay_log": draw_decay_log(jax.random.fold_in(arg_keys[5], 71), 0),
    }


EPSILON = 1e-05

def reference(fine_rows, w_inputs, w_out, head_gain, decay_log):
    head_dim = D // ATTENDER_NUMBER
    blocks = POOLED_SPAN // CH
    widened = jnp.concatenate([jnp.zeros((SF - 1, D), jnp.float32), fine_rows[:LF - (SF - 1)].astype(jnp.float32)], axis=0)
    pooled = lax.optimization_barrier(jnp.mean(widened.reshape(POOLED_SPAN, SF, D), axis=1)).astype(jnp.bfloat16)

    def project(slot_number):
        return jnp.dot(pooled, w_inputs[:, slot_number, :], preferred_element_type=jnp.float32)
    queries = project(0).astype(jnp.bfloat16).reshape(blocks, CH, ATTENDER_NUMBER, head_dim)
    key_rows = project(1).astype(jnp.bfloat16).reshape(blocks, CH, ATTENDER_NUMBER, head_dim)
    values = project(2).astype(jnp.bfloat16).reshape(blocks, CH, ATTENDER_NUMBER, head_dim)
    gate_values = project(3)
    decays = decay_log.reshape(ATTENDER_NUMBER, blocks, CH).transpose(1, 0, 2)
    causal = jnp.arange(CH)[:, None] >= jnp.arange(CH)[None, :]

    def advance(state, inputs):
        query_block, key_block, value_block, decay_block = inputs
        cumulative = jnp.cumsum(decay_block, axis=1)
        gaps = cumulative[:, :, None] - cumulative[:, None, :]
        weight = jnp.where(causal, jnp.exp(jnp.minimum(gaps, 0.0)), 0.0)
        scores = jnp.einsum('thd,shd->hts', query_block.astype(jnp.float32), key_block.astype(jnp.float32)) * weight
        scores = lax.optimization_barrier(scores.astype(jnp.bfloat16)).astype(jnp.float32)
        within = jnp.einsum('hts,shd->thd', scores, value_block.astype(jnp.float32))
        rounded = lax.optimization_barrier(state.astype(jnp.bfloat16)).astype(jnp.float32)
        summed = jnp.einsum('thd,hde->the', query_block.astype(jnp.float32), rounded) * jnp.exp(cumulative).T[:, :, None]
        remaining = jnp.exp(cumulative[:, -1:] - cumulative)
        decayed = (key_block.astype(jnp.float32) * remaining.T[:, :, None]).astype(jnp.bfloat16)
        decayed = lax.optimization_barrier(decayed).astype(jnp.float32)
        new_state = jnp.exp(cumulative[:, -1])[:, None, None] * state + jnp.einsum('shd,she->hde', decayed, value_block.astype(jnp.float32))
        return (new_state, within + summed)
    initial = jnp.zeros((ATTENDER_NUMBER, head_dim, head_dim), jnp.float32)
    _, attended = lax.scan(advance, initial, (queries, key_rows, values, decays))
    attended = attended.reshape(POOLED_SPAN, ATTENDER_NUMBER, head_dim)
    square_mean = lax.optimization_barrier(jnp.mean(attended * attended, axis=2, keepdims=True))
    normed = (attended * lax.rsqrt(square_mean + EPSILON)).reshape(POOLED_SPAN, D)
    gated_rows = (normed * head_gain * jax.nn.silu(gate_values)).astype(jnp.bfloat16)
    group_width = HEADS_DEV * head_dim
    coarse = jnp.zeros((POOLED_SPAN, D), jnp.float32)
    for group_index in range(N_MP):
        group_term = jnp.dot(gated_rows[:, group_index * group_width:(group_index + 1) * group_width], w_out[group_index * group_width:(group_index + 1) * group_width], preferred_element_type=jnp.float32)
        coarse = coarse + lax.optimization_barrier(group_term.astype(jnp.bfloat16)).astype(jnp.float32)
    return (fine_rows.astype(jnp.float32) + jnp.repeat(coarse, SF, axis=0)).astype(jnp.bfloat16)
```

```python
import jax
import jax.numpy as jnp
from jax import lax
from jax.experimental import pallas as pl
from jax.experimental.pallas import tpu as pltpu
from jax.sharding import PartitionSpec as P

D = 4096
ATTENDER_NUMBER = 32
SF = 4
CH = 128
HD = D // ATTENDER_NUMBER


EPSILON = 1e-05
BF = jnp.bfloat16
F32 = jnp.float32
VMEM_LIMIT = 48 * 2**20


def passed_along(value, axis, by):
    peers = lax.axis_size(axis)
    pairs = [(i, i + by) for i in range(peers) if 0 <= i + by < peers]
    return lax.ppermute(value, axis, pairs)


def swapped(value, axis, bit):
    peers = lax.axis_size(axis)
    return lax.ppermute(value, axis, [(i, i ^ bit) for i in range(peers)])


def params(**kw):
    return pltpu.CompilerParams(vmem_limit_bytes=VMEM_LIMIT, **kw)


def cost(flops, size):
    return pl.CostEstimate(flops=int(flops), bytes_accessed=int(size), transcendentals=0)


def dot(a, b):
    return jnp.dot(a, b, preferred_element_type=F32)


def dot_dims(a, b, da, db):
    return lax.dot_general(a, b, (((da,), (db,)), ((), ())), preferred_element_type=F32)


def pool_half(fine, tail, block, tail_block):
    rows, width = fine.shape[0] // 2, fine.shape[1]
    out_rows, cols = rows // SF, min(width, 1024)

    def kernel(tail_ref, fine_ref, out_ref):
        j = lax.broadcasted_iota(jnp.int32, (out_rows, rows), 0) * SF
        i = lax.broadcasted_iota(jnp.int32, (out_rows, rows), 1)
        main = jnp.where((i <= j) & (i > j - SF), 1.0 / SF, 0.0).astype(BF)
        jt = lax.broadcasted_iota(jnp.int32, (out_rows, 16), 0) * SF
        it = lax.broadcasted_iota(jnp.int32, (out_rows, 16), 1) - 16
        ahead = jnp.where((it <= jt) & (it > jt - SF), 1.0 / SF, 0.0).astype(BF)
        total = dot(main, fine_ref[...]) + dot(ahead, tail_ref[...])
        out_ref[...] = total.astype(BF)

    return pl.pallas_call(
        kernel,
        grid=(width // cols,),
        in_specs=[
            pl.BlockSpec((16, cols), lambda c: (tail_block, c)),
            pl.BlockSpec((rows, cols), lambda c: (block, c)),
        ],
        out_specs=pl.BlockSpec((out_rows, cols), lambda c: (0, c)),
        out_shape=jax.ShapeDtypeStruct((out_rows, width), BF),
        compiler_params=params(),
        cost_estimate=cost(2 * out_rows * rows * width, 2 * rows * width),
    )(tail, fine)


def project(pieces, weights, firsts, width):
    piece_rows, depth = pieces[0].shape
    count, rows, cols = len(pieces), len(pieces) * pieces[0].shape[0], 256
    per = width // cols
    ranges = len(firsts)

    def kernel(*refs):
        ins, w_ref, outs, held = refs[:count], refs[count], refs[count + 1 : count + 1 + ranges], refs[-1]
        step = pl.program_id(0)

        @pl.when(step == 0)
        def _():
            for n in range(count):
                held[n * piece_rows : (n + 1) * piece_rows] = ins[n][...]

        result = dot(held[...], w_ref[...])
        for n in range(ranges):

            @pl.when(step // per == n)
            def _():
                outs[n][...] = result.astype(outs[n].dtype)

    def w_index(step):
        block = firsts[0] // cols + step % per
        for n in range(1, ranges):
            block = jnp.where(step // per == n, firsts[n] // cols + step % per, block)
        return (0, block)

    def out_index(n):
        return lambda step: (0, jnp.clip(step - n * per, 0, per - 1))

    return pl.pallas_call(
        kernel,
        grid=(ranges * per,),
        in_specs=[pl.BlockSpec((piece_rows, depth), lambda step: (0, 0))] * count
        + [pl.BlockSpec((depth, cols), w_index)],
        out_specs=[pl.BlockSpec((rows, cols), out_index(n)) for n in range(ranges)],
        out_shape=[
            jax.ShapeDtypeStruct((rows, width), F32 if n == ranges - 1 else BF) for n in range(ranges)
        ],
        scratch_shapes=[pltpu.VMEM((rows, depth), BF)],
        compiler_params=params(),
        cost_estimate=cost(2 * rows * depth * width * ranges, 2 * depth * width * ranges),
    )(*pieces, weights)


def natural_units(me):
    x, y, d = me ^ 1, me ^ 2, me ^ 3
    return [2 * me, 2 * me + 1, 2 * x, 2 * y + 1, 2 * x + 1, 2 * y, 2 * d, 2 * d + 1]


def last_keys_and_state(me, pieces, weights, first, second, cum_columns, width):
    unit, depth = pieces[0].shape
    rows = 8 * unit
    cols = 2 * HD
    per = width // cols
    heads = cum_columns.shape[1]

    def kernel(me_ref, d0, d1, wk_ref, wv_ref, k1, v1, k2, v2, cum_ref, k_out, v_out, s_out, held, keys, vals):
        step = pl.program_id(0)

        @pl.when(step == 0)
        def _():
            held[:unit] = d0[...]
            held[unit:] = d1[...]

        k_last = dot(held[...], wk_ref[...]).astype(BF)
        v_last = dot(held[...], wv_ref[...]).astype(BF)
        k_out[...] = k_last
        v_out[...] = v_last
        order = natural_units(me_ref[0])
        total = cum_ref[rows - 1 : rows, :]
        lane = lax.broadcasted_iota(jnp.int32, (unit, heads), 1)
        for n, natural in enumerate(order):
            cum = cum_ref[pl.ds(pl.multiple_of(natural * unit, unit), unit), :]
            left = jnp.exp(total - cum)
            if n < 4:
                part = k1[n * unit : (n + 1) * unit]
            elif n < 6:
                part = k2[(n - 4) * unit : (n - 3) * unit]
            else:
                part = k_last[(n - 6) * unit : (n - 5) * unit]
            for h in range(2):
                scale = jnp.sum(jnp.where(lane == 2 * step + h, left, 0.0), axis=1, keepdims=True)
                keys[n * unit : (n + 1) * unit, h * HD : (h + 1) * HD] = (
                    part[:, h * HD : (h + 1) * HD].astype(F32) * scale
                ).astype(BF)
        vals[: 4 * unit] = v1[...]
        vals[4 * unit : 6 * unit] = v2[...]
        vals[6 * unit :] = v_last
        both = dot_dims(keys[...], vals[...], 0, 0)
        for h in range(2):
            s_out[h * HD : (h + 1) * HD] = both[h * HD : (h + 1) * HD, h * HD : (h + 1) * HD].astype(BF)

    def column(block_rows, offset=0):
        return pl.BlockSpec((block_rows, cols), lambda step, me: (0, offset + step))

    whole = lambda step, me: (0, 0)
    return pl.pallas_call(
        kernel,
        grid_spec=pltpu.PrefetchScalarGridSpec(
            num_scalar_prefetch=1,
            grid=(per,),
            in_specs=[pl.BlockSpec((unit, depth), whole)] * 2
            + [column(depth, per), column(depth, 2 * per)]
            + [column(4 * unit), column(4 * unit), column(2 * unit), column(2 * unit)]
            + [pl.BlockSpec((rows, heads), whole)],
            out_specs=[column(2 * unit), column(2 * unit), pl.BlockSpec((cols, HD), lambda step, me: (step, 0))],
            scratch_shapes=[
                pltpu.VMEM((2 * unit, depth), BF),
                pltpu.VMEM((rows, cols), BF),
                pltpu.VMEM((rows, cols), BF),
            ],
        ),
        out_shape=[
            jax.ShapeDtypeStruct((2 * unit, width), BF),
            jax.ShapeDtypeStruct((2 * unit, width), BF),
            jax.ShapeDtypeStruct((width, HD), BF),
        ],
        compiler_params=params(),
        cost_estimate=cost(4 * 2 * unit * depth * width, 4 * depth * width),
    )(me, *pieces, weights, weights, first[1], first[2], second[1], second[2], cum_columns)


def local_attention(me, firsts, seconds, lasts, gain, cum_columns, cum_rows, width):
    unit = lasts[0].shape[0] // 2
    rows = 8 * unit
    cols = 2 * HD
    heads = cum_columns.shape[1]
    blocks = rows // CH

    def kernel(
        me_ref, q1, k1, v1, g1, q2, k2, v2, g2, q3, k3, v3, g3, gain_ref, cc_ref, cr_ref,
        a1, s1, z1, a2, s2, z2, a3, s3, z3, q, k, v, a, s,
    ):
        step = pl.program_id(0)
        order = natural_units(me_ref[0])
        places = [pl.ds(pl.multiple_of(n * unit, unit), unit) for n in order]
        for to, parts in ((q, (q1, q2, q3)), (k, (k1, k2, k3)), (v, (v1, v2, v3))):
            for n, place in enumerate(places):
                part, at = (parts[0], n) if n < 4 else (parts[1], n - 4) if n < 6 else (parts[2], n - 6)
                to[place, :] = part[at * unit : (at + 1) * unit, :]
        lane = lax.broadcasted_iota(jnp.int32, (rows, heads), 1)
        sub = lax.broadcasted_iota(jnp.int32, (heads, rows), 0)
        causal = lax.broadcasted_iota(jnp.int32, (CH, CH), 0) >= lax.broadcasted_iota(jnp.int32, (CH, CH), 1)
        for h in range(2):
            here = slice(h * HD, (h + 1) * HD)
            column = jnp.sum(jnp.where(lane == 2 * step + h, cc_ref[...], 0.0), axis=1, keepdims=True)
            row = jnp.sum(jnp.where(sub == 2 * step + h, cr_ref[...], 0.0), axis=0, keepdims=True)
            s[:, here] = (q[:, here].astype(F32) * jnp.exp(column)).astype(BF)
            state = jnp.zeros((HD, HD), F32)
            for b in range(blocks):
                t = slice(b * CH, (b + 1) * CH)
                qb, kb, vb = q[t, here], k[t, here], v[t, here]
                ct, cs = column[t], row[:, t]
                before = column[b * CH - 1 : b * CH] if b else jnp.zeros((1, 1), F32)
                end = column[(b + 1) * CH - 1 : (b + 1) * CH]
                weight = jnp.where(causal, jnp.exp(jnp.minimum(ct - cs, 0.0)), 0.0)
                scores = (dot_dims(qb, kb, 1, 1) * weight).astype(BF)
                within = dot(scores, vb)
                if b:
                    within = within + dot(qb, state.astype(BF)) * jnp.exp(ct - before)
                a[t, here] = within
                if b < blocks - 1:
                    decayed = (kb.astype(F32) * jnp.exp(end - ct)).astype(BF)
                    state = jnp.exp(end - before) * state + dot_dims(decayed, vb, 0, 0)
        for n, place in enumerate(places):
            to_a, to_s, at = (a1, s1, n) if n < 4 else (a2, s2, n - 4) if n < 6 else (a3, s3, n - 6)
            to_a[at * unit : (at + 1) * unit, :] = a[place, :]
            to_s[at * unit : (at + 1) * unit, :] = s[place, :]
        for g, z in ((g1, z1), (g2, z2), (g3, z3)):
            gate = g[...]
            z[...] = gain_ref[...] * (gate / (1.0 + jnp.exp(-gate)))

    def column(block_rows):
        return pl.BlockSpec((block_rows, cols), lambda step, me: (0, step))

    whole = lambda step, me: (0, 0)
    counts = (4 * unit, 2 * unit, 2 * unit)
    outs = pl.pallas_call(
        kernel,
        grid_spec=pltpu.PrefetchScalarGridSpec(
            num_scalar_prefetch=1,
            grid=(width // cols,),
            in_specs=[column(n) for n in counts for _ in range(4)]
            + [column(1), pl.BlockSpec((rows, heads), whole), pl.BlockSpec((heads, rows), whole)],
            out_specs=[column(n) for n in counts for _ in range(3)],
            scratch_shapes=[pltpu.VMEM((rows, cols), BF)] * 3
            + [pltpu.VMEM((rows, cols), F32), pltpu.VMEM((rows, cols), BF)],
        ),
        out_shape=[jax.ShapeDtypeStruct((n, width), t) for n in counts for t in (F32, BF, F32)],
        compiler_params=params(),
        cost_estimate=cost(10 * rows * CH * width, 30 * rows * width),
    )(me, *firsts, *seconds, *lasts, gain, cum_columns, cum_rows)
    return outs[:3], outs[3:6], outs[6:]


def weighted_sum(terms, factors):
    rows = terms[0].shape[0]
    heads = rows // HD

    def kernel(*refs):
        ins, f_ref, out_ref = refs[: len(terms)], refs[len(terms)], refs[-1]
        for h in range(heads):
            here = slice(h * HD, (h + 1) * HD)
            total = None
            for n, ref in enumerate(ins):
                term = ref[here].astype(F32) * f_ref[n, h : h + 1, :]
                total = term if total is None else total + term
            out_ref[here] = total.astype(BF)

    return pl.pallas_call(
        kernel,
        out_shape=jax.ShapeDtypeStruct((rows, HD), BF),
        compiler_params=params(),
        cost_estimate=cost(2 * len(terms) * rows * HD, 2 * (len(terms) + 1) * rows * HD),
    )(*terms, factors)


def entering_state(state, totals):
    peers = lax.axis_size("seq")
    rank = lax.axis_index("seq")
    heads = totals.shape[1]
    half = heads // 2
    core, chip = rank % 2, rank // 2
    chips = peers // 2
    one = jnp.ones((half, HD), F32)
    own_half = lambda value: lax.dynamic_slice_in_dim(value, core * half, half, 0)
    total_of = lambda r: lax.dynamic_index_in_dim(totals, jnp.clip(r, 0, peers - 1), 0, keepdims=False)
    later = jnp.exp(own_half(total_of(2 * chip + 1)))
    factors = jnp.stack([jnp.where(core == 0, later, one), jnp.where(core == 0, one, later)])
    weights = []
    passed = jnp.zeros((half, HD), F32)
    for d in range(1, chips):
        weights.append(jnp.where(chip >= d, jnp.exp(passed), 0.0))
        passed = passed + own_half(total_of(2 * (chip - d)) + total_of(2 * (chip - d) + 1))
    weights = jnp.stack(weights)
    first_decay = jnp.exp(total_of(2 * chip))
    final = jnp.stack(
        [
            jnp.where(core == 0, 1.0, first_decay),
            jnp.where(core == 0, 0.0, jnp.ones_like(first_decay)),
        ]
    )
    factors, weights, final = lax.optimization_barrier((factors, weights, final))

    other = swapped(state, "seq", 1)
    size = half * HD
    mine = lax.dynamic_slice_in_dim(state, core * size, size, 0)
    theirs = lax.dynamic_slice_in_dim(other, core * size, size, 0)
    chip_state = weighted_sum([mine, theirs], factors)
    arrived = [passed_along(chip_state, "seq", 2 * d) for d in range(1, chips)]
    entering = weighted_sum(arrived, weights)
    entering_other = swapped(entering, "seq", 1)
    low = jnp.where(core == 0, entering, entering_other)
    high = jnp.where(core == 0, entering_other, entering)
    return weighted_sum([jnp.concatenate([low, high]), other], final)


def output_terms(parts, incoming, w_out):
    unit = parts[0][0].shape[0] // parts[0][4]
    width, model = w_out.shape
    cols = model // 4
    heads = width // HD

    def kernel(a0, s0, z0, a1, s1, z1, in_ref, w_ref, out_a, out_b, gated):
        step = pl.program_id(0)

        @pl.when(step == 0)
        def _():
            for n, (a, s, z) in enumerate(((a0, s0, z0), (a1, s1, z1))):
                for h in range(heads):
                    here = slice(h * HD, (h + 1) * HD)
                    attended = a[:, here] + dot(s[:, here], in_ref[here])
                    mean = jnp.mean(attended * attended, axis=1, keepdims=True)
                    gated[n * unit : (n + 1) * unit, here] = (
                        attended * lax.rsqrt(mean + EPSILON) * z[:, here]
                    ).astype(BF)

        result = dot(gated[...], w_ref[...]).astype(BF)

        @pl.when(step < 2)
        def _():
            out_a[...] = result

        @pl.when(step >= 2)
        def _():
            out_b[...] = result

    specs, args = [], []
    for a, s, z, block, _ in parts:
        specs += [pl.BlockSpec((unit, width), lambda step, block=block: (block, 0))] * 3
        args += [a, s, z]
    return pl.pallas_call(
        kernel,
        grid=(4,),
        in_specs=specs
        + [
            pl.BlockSpec((width, HD), lambda step: (0, 0)),
            pl.BlockSpec((width, cols), lambda step: (0, step)),
        ],
        out_specs=[
            pl.BlockSpec((2 * unit, cols), lambda step: (0, jnp.minimum(step, 1))),
            pl.BlockSpec((2 * unit, cols), lambda step: (0, jnp.maximum(step - 2, 0))),
        ],
        out_shape=[jax.ShapeDtypeStruct((2 * unit, model // 2), BF)] * 2,
        scratch_shapes=[pltpu.VMEM((2 * unit, width), BF)],
        compiler_params=params(),
        cost_estimate=cost(4 * unit * width * model, 2 * width * model),
    )(*args, incoming, w_out)


def merged(own, arrived, quarter):
    rows, cols = own.shape[0], own.shape[1] // 2

    def kernel(a, b, out):
        out[...] = (a[...].astype(F32) + b[...].astype(F32)).astype(BF)

    spec = pl.BlockSpec((rows, cols), lambda step: (0, quarter))
    return pl.pallas_call(
        kernel,
        grid=(1,),
        in_specs=[spec, spec],
        out_specs=pl.BlockSpec((rows, cols), lambda step: (0, 0)),
        out_shape=jax.ShapeDtypeStruct((rows, cols), BF),
        compiler_params=params(),
        cost_estimate=cost(rows * cols, 6 * rows * cols),
    )(own, arrived)


def add_coarse(fine, columns, previous=None):
    rows, model = fine.shape
    cols = model // 4
    pieces = 3
    tall = rows // pieces
    coarse = tall // SF
    quarters = [quarter for quarter, _ in columns]
    flat = [term for _, terms in columns for term in terms]

    def kernel(*refs):
        fine_ref, terms, out_ref = refs[0], refs[1 : 1 + len(flat)], refs[-1]
        r = lax.broadcasted_iota(jnp.int32, (tall, coarse), 0) // SF
        c = lax.broadcasted_iota(jnp.int32, (tall, coarse), 1)
        spread = jnp.where(r == c, 1.0, 0.0).astype(BF)
        for n in range(len(columns)):

            @pl.when(pl.program_id(0) == n)
            def _():
                total = fine_ref[...].astype(F32)
                for term in terms[3 * n : 3 * n + 3]:
                    total += dot(spread, term[...])
                out_ref[...] = total.astype(BF)

    def where(step):
        return jnp.where(step == 0, quarters[0], quarters[1])

    fine_spec = pl.BlockSpec((tall, cols), lambda step, piece: (piece, where(step)))
    specs = [fine_spec]
    for n, (_, terms) in enumerate(columns):
        for _, block in terms:
            last = pieces - 1
            if n == 0:
                index = lambda step, piece, block=block: (jnp.where(step == 0, piece, last), block)
            else:
                index = lambda step, piece, block=block: (jnp.where(step == 0, 0, piece), block)
            specs.append(pl.BlockSpec((coarse, cols), index))
    args = [fine] + [term for term, _ in flat]
    aliases = {}
    if previous is not None:
        specs.append(pl.BlockSpec(memory_space=pl.ANY))
        args.append(previous)
        aliases = {len(args) - 1: 0}
    return pl.pallas_call(
        kernel,
        grid=(2, pieces),
        in_specs=specs,
        out_specs=fine_spec,
        out_shape=jax.ShapeDtypeStruct((rows, model), BF),
        input_output_aliases=aliases,
        compiler_params=params(),
        cost_estimate=cost(6 * rows * coarse * cols, 4 * rows * cols),
    )(*args)


def body_square(fine_rows, w_inputs, w_out, head_gain, decay_log):
    model = fine_rows.shape[1]
    fine_count = fine_rows.shape[0]
    heads, rows_coarse = decay_log.shape
    width = heads * HD
    me = lax.axis_index("mp")
    place = jnp.reshape(me, (1,)).astype(jnp.int32)

    before = passed_along(fine_rows[fine_count - 16 :], ("seq", "mp"), 1)
    weights = w_inputs.reshape(model, 4 * width)
    cum_rows = jnp.cumsum(decay_log, axis=1)
    cum_columns = cum_rows.T
    totals = lax.all_gather(
        jnp.broadcast_to(cum_rows[:, -1:], (heads, HD))[None], "seq", axis=0, tiled=True
    )

    p1 = pool_half(fine_rows, fine_rows, 1, fine_count // 32 - 1)
    p0 = pool_half(fine_rows, before, 0, 0)
    y1 = swapped(p1, "mp", 2)
    x0 = swapped(p0, "mp", 1)
    y0 = swapped(p0, "mp", 2)
    x1 = swapped(p1, "mp", 1)
    d0 = swapped(x0, "mp", 2)
    d1 = swapped(y1, "mp", 1)

    everything = [0, width, 2 * width, 3 * width]
    first = project([p0, p1, x0, y1], weights, everything, width)
    second = project([x1, y0], weights, everything, width)
    k_last, v_last, state = last_keys_and_state(place, [d0, d1], weights, first, second, cum_columns, width)
    q_last, g_last = project([d0, d1], weights, [0, 3 * width], width)
    a1, a2, a3 = local_attention(
        place, first, second, [q_last, k_last, v_last, g_last], head_gain[None], cum_columns, cum_rows, width
    )
    incoming = entering_state(state, totals)

    n = 4
    far_a, far_b = output_terms([(*a3, 0, 2), (*a3, 1, 2)], incoming, w_out)
    got_a = swapped(far_a, "mp", 1)
    got_b = swapped(far_b, "mp", 2)
    x_a, x_b = output_terms([(*a1, 2, n), (*a2, 0, 2)], incoming, w_out)
    from_x_a = swapped(x_a, "mp", 1)
    y_a, y_b = output_terms([(*a2, 1, 2), (*a1, 3, n)], incoming, w_out)
    from_y_b = swapped(y_b, "mp", 2)
    own_a, own_b = output_terms([(*a1, 0, n), (*a1, 1, n)], incoming, w_out)
    from_x_b = [swapped(merged(x_b, got_b, q), "mp", 1) for q in range(2)]
    from_y_a = [swapped(merged(y_a, got_a, q), "mp", 2) for q in range(2)]
    out = None
    for q in range(2):
        out = add_coarse(
            fine_rows,
            [
                (q, [(own_a, q), (from_x_a, q), (from_y_a[q], 0)]),
                (2 + q, [(own_b, q), (from_y_b, q), (from_x_b[q], 0)]),
            ],
            out,
        )
    return out


def body(fine_rows, w_inputs, w_out, head_gain, decay_log):
    model_width = fine_rows.shape[1]
    head_dim = D // ATTENDER_NUMBER
    local_heads = decay_log.shape[0]
    local_width = local_heads * head_dim
    rows_coarse = decay_log.shape[1]
    blocks = rows_coarse // CH
    fine_count = fine_rows.shape[0]
    tail_rows = fine_rows[fine_count - (SF - 1) :]
    before = passed_along(tail_rows, ("seq", "mp"), 1)
    widened = jnp.concatenate([before, fine_rows[: fine_count - (SF - 1)]], axis=0).astype(
        jnp.float32
    )
    pooled = jnp.mean(widened.reshape(-1, SF, model_width), axis=1).astype(jnp.bfloat16)
    weights_flat = w_inputs.reshape(model_width, 4 * local_width)
    projected = jnp.dot(
        lax.all_gather(pooled, "mp", axis=0, tiled=True),
        weights_flat,
        preferred_element_type=jnp.float32,
    )
    queries = (
        projected[:, :local_width].astype(jnp.bfloat16).reshape(blocks, CH, local_heads, head_dim)
    )
    key_rows = (
        projected[:, local_width : 2 * local_width]
        .astype(jnp.bfloat16)
        .reshape(blocks, CH, local_heads, head_dim)
    )
    values = (
        projected[:, 2 * local_width : 3 * local_width]
        .astype(jnp.bfloat16)
        .reshape(blocks, CH, local_heads, head_dim)
    )
    gate_values = projected[:, 3 * local_width :]
    cumulative = jnp.cumsum(decay_log.reshape(local_heads, blocks, CH), axis=2)
    gaps = cumulative[:, :, :, None] - cumulative[:, :, None, :]
    causal = jnp.arange(CH)[:, None] >= jnp.arange(CH)[None, :]
    weight = jnp.where(causal, jnp.exp(jnp.minimum(gaps, 0.0)), 0.0)
    scores = jnp.einsum("cthd,cshd->hcts", queries, key_rows, preferred_element_type=jnp.float32)
    scores = (scores * weight).astype(jnp.bfloat16)
    within = jnp.einsum("hcts,cshd->cthd", scores, values, preferred_element_type=jnp.float32)
    remaining = jnp.exp(cumulative[:, :, -1:] - cumulative)
    decayed_keys = (
        key_rows.astype(jnp.float32) * jnp.transpose(remaining, (1, 2, 0))[..., None]
    ).astype(jnp.bfloat16)
    block_states = jnp.einsum(
        "cshd,cshe->chde", decayed_keys, values, preferred_element_type=jnp.float32
    )
    block_decay = cumulative[:, :, -1]
    prefix_states = []
    prefix_decay = []
    running = jnp.zeros((local_heads, head_dim, head_dim), jnp.float32)
    decay_total = jnp.zeros((local_heads,), jnp.float32)
    for block_index in range(blocks):
        prefix_states.append(running)
        prefix_decay.append(decay_total)
        running = (
            jnp.exp(block_decay[:, block_index])[:, None, None] * running
            + block_states[block_index]
        )
        decay_total = decay_total + block_decay[:, block_index]
    shard_totals = lax.all_gather(decay_total[None, :], "seq", axis=0, tiled=True)
    my_rank = lax.axis_index("seq")
    running_ends = jnp.cumsum(shard_totals, axis=0)
    before_mine = lax.dynamic_slice_in_dim(running_ends - shard_totals, my_rank, 1, 0)
    shard_states = lax.all_gather(
        running[None].astype(jnp.bfloat16), "seq", axis=0, tiled=True
    ).astype(jnp.float32)
    row_count = shard_states.shape[0]
    span_sums = before_mine - running_ends
    device_rank = jnp.arange(row_count, dtype=jnp.int32)
    factor = jnp.where((device_rank < my_rank)[:, None], jnp.exp(jnp.minimum(span_sums, 0.0)), 0.0)
    incoming = jnp.zeros_like(running) + jnp.sum(factor[:, :, None, None] * shard_states, axis=0)
    entering = jnp.stack(
        [
            jnp.exp(prefix_decay[block_index])[:, None, None] * incoming
            + prefix_states[block_index]
            for block_index in range(blocks)
        ]
    )
    carried = jnp.einsum(
        "cthd,chde->cthe",
        queries,
        entering.astype(jnp.bfloat16),
        preferred_element_type=jnp.float32,
    )
    carried = carried * jnp.transpose(jnp.exp(cumulative), (1, 2, 0))[..., None]
    attended = (within + carried).reshape(rows_coarse, local_heads, head_dim)
    square_mean = jnp.mean(attended * attended, axis=2, keepdims=True)
    normed = (attended * lax.rsqrt(square_mean + EPSILON)).reshape(rows_coarse, local_width)
    gated_rows = (normed * head_gain * jax.nn.silu(gate_values)).astype(jnp.bfloat16)
    coarse = lax.psum_scatter(
        jnp.dot(gated_rows, w_out, preferred_element_type=jnp.float32).astype(jnp.bfloat16),
        "mp",
        scatter_dimension=0,
        tiled=True,
    ).astype(jnp.float32)
    upsampled = jnp.repeat(coarse, SF, axis=0)
    return (fine_rows.astype(jnp.float32) + upsampled).astype(jnp.bfloat16)


def solution(mesh):
    square = mesh.shape["mp"] == 4 and mesh.shape["seq"] % 2 == 0 and mesh.shape["seq"] > 2
    return jax.shard_map(
        body_square if square else body,
        mesh=mesh,
        in_specs=(
            P(("seq", "mp"), None),
            P(None, None, "mp"),
            P("mp", None),
            P("mp"),
            P("mp", "seq"),
        ),
        out_specs=P(("seq", "mp"), None),
        check_vma=False,
    )
```

```python
import jax
import jax.numpy as jnp
from jax import lax
from jax.experimental import pallas as pl
from jax.experimental.pallas import tpu as pltpu
from jax.sharding import PartitionSpec as P

D = 4096
ATTENDER_NUMBER = 32
SF = 4
CH = 128
HD = D // ATTENDER_NUMBER


EPSILON = 1e-05
BF = jnp.bfloat16
F32 = jnp.float32
MIB = 2**20
SMALL = 14 * MIB
ANY = pl.BlockSpec(memory_space=pl.ANY)
VMEM = pl.BlockSpec(memory_space=pltpu.VMEM)
SMEM = pl.BlockSpec(memory_space=pltpu.SMEM)


def passed_along(value, axis, by):
    peers = lax.axis_size(axis)
    pairs = [(i, i + by) for i in range(peers) if 0 <= i + by < peers]
    return lax.ppermute(value, axis, pairs)


def swapped(value, axis, bit):
    peers = lax.axis_size(axis)
    return lax.ppermute(value, axis, [(i, i ^ bit) for i in range(peers)])


def params(limit):
    return pltpu.CompilerParams(vmem_limit_bytes=limit)


def in_vmem(*arrays):
    return [pltpu.with_memory_space_constraint(array, pltpu.VMEM) for array in arrays]


def cost(flops, size):
    return pl.CostEstimate(flops=int(flops), bytes_accessed=int(size), transcendentals=0)


def dot(a, b):
    return jnp.dot(a, b, preferred_element_type=F32)


def dot_dims(a, b, da, db):
    return lax.dot_general(a, b, (((da,), (db,)), ((), ())), preferred_element_type=F32)


def pool_half(fine, tail, first, tail_first):
    rows, width = fine.shape[0] // 2, fine.shape[1]
    out_rows, parts = rows // SF, 4
    cols = width // parts

    def kernel(tail_ref, fine_ref, out_ref, ahead_rows, main_rows, pooled, tail_sem, fine_sems, out_sems):
        here = [pl.ds(n * cols, cols) for n in range(parts)]
        tail_copy = pltpu.make_async_copy(tail_ref.at[pl.ds(tail_first, 16)], ahead_rows, tail_sem)
        copies = [
            pltpu.make_async_copy(fine_ref.at[pl.ds(first, rows), c], main_rows.at[:, c], fine_sems.at[n])
            for n, c in enumerate(here)
        ]
        tail_copy.start()
        for copy in copies:
            copy.start()
        j = lax.broadcasted_iota(jnp.int32, (out_rows, rows), 0) * SF
        i = lax.broadcasted_iota(jnp.int32, (out_rows, rows), 1)
        main = jnp.where((i <= j) & (i > j - SF), 1.0 / SF, 0.0).astype(BF)
        jt = lax.broadcasted_iota(jnp.int32, (out_rows, 16), 0) * SF
        it = lax.broadcasted_iota(jnp.int32, (out_rows, 16), 1) - 16
        ahead = jnp.where((it <= jt) & (it > jt - SF), 1.0 / SF, 0.0).astype(BF)
        tail_copy.wait()
        outs = []
        for n, c in enumerate(here):
            copies[n].wait()
            total = dot(main, main_rows[:, c]) + dot(ahead, ahead_rows[:, c])
            pooled[:, c] = total.astype(BF)
            outs.append(pltpu.make_async_copy(pooled.at[:, c], out_ref.at[:, c], out_sems.at[n]))
            outs[n].start()
        for copy in outs:
            copy.wait()

    return pl.pallas_call(
        kernel,
        in_specs=[ANY, ANY],
        out_specs=ANY,
        out_shape=jax.ShapeDtypeStruct((out_rows, width), BF),
        scratch_shapes=[
            pltpu.VMEM((16, width), BF),
            pltpu.VMEM((rows, width), BF),
            pltpu.VMEM((out_rows, width), BF),
            pltpu.SemaphoreType.DMA,
            pltpu.SemaphoreType.DMA((parts,)),
            pltpu.SemaphoreType.DMA((parts,)),
        ],
        compiler_params=params(58 * MIB),
        cost_estimate=cost(2 * out_rows * rows * width, 2 * rows * width),
    )(tail, fine)


def prepare(raw, *after):
    depth, kinds, width = raw.shape
    lanes = 128
    tiles = width // lanes
    per = kinds * tiles
    rows = raw.reshape(depth, kinds, tiles, lanes).transpose(0, 2, 1, 3).reshape(depth * per, lanes)
    bk, slots, size = 256, 4, 8 * per
    steps = depth // bk

    def kernel(raw_ref, *refs):
        w_refs, (buf, sems) = refs[-2 - kinds : -2], refs[-2:]


        def fetch(step, slot):
            return pltpu.make_async_copy(
                raw_ref.at[pl.ds(pl.multiple_of(step * bk * per, bk * per), bk * per)], buf.at[slot], sems.at[slot]
            )

        for n in range(slots):
            fetch(n, n).start()
        to = lax.broadcasted_iota(jnp.int32, (size, size), 0)
        of = lax.broadcasted_iota(jnp.int32, (size, size), 1)
        order = jnp.where(of == (to % 8) * per + to // 8, 1.0, 0.0).astype(BF)

        def loop(step, carry):
            slot = lax.rem(step, slots)
            fetch(step, slot).wait()

            def sixteen(i, carry):
                start = pl.multiple_of(i * 2 * size, 2 * size)
                low, high = buf[slot, pl.ds(start, size)], buf[slot, pl.ds(start + size, size)]
                moved = dot(order, jnp.concatenate([low, high], axis=1))
                k = pl.ds(pl.multiple_of(step * bk + i * 16, 16), 16)
                for q in range(per):
                    eight = moved[q * 8 : (q + 1) * 8]
                    w_refs[q % kinds][k, (q // kinds) * lanes : (q // kinds + 1) * lanes] = jnp.concatenate(
                        [eight[:, :lanes], eight[:, lanes:]], axis=0
                    ).astype(BF)
                return carry

            lax.fori_loop(0, bk // 16, sixteen, 0, unroll=4)

            @pl.when(step + slots < steps)
            def _():
                fetch(step + slots, slot).start()

            return carry

        lax.fori_loop(0, steps, loop, 0)

    return pl.pallas_call(
        kernel,
        in_specs=[ANY] * (1 + len(after)),
        out_specs=[VMEM] * kinds,
        out_shape=[pltpu.VMEM((depth, width), BF)] * kinds,
        scratch_shapes=[pltpu.VMEM((slots, bk * per, lanes), BF), pltpu.SemaphoreType.DMA((slots,))],
        compiler_params=params(10 * MIB),
        cost_estimate=cost(2 * depth * kinds * width * size, 4 * depth * kinds * width),
    )(rows, *after)


def project(pieces, weights, types):
    unit, depth = pieces[0].shape
    rows, width, cols = 2 * unit, weights[0].shape[1], 512
    count = len(weights)

    def kernel(d0, d1, *refs):
        w_refs, outs, held = refs[:count], refs[count : 2 * count], refs[-1]
        held[:unit] = d0[...]
        held[unit:] = d1[...]
        for n in range(count):
            for c in range(0, width, cols):
                outs[n][:, c : c + cols] = dot(held[...], w_refs[n][:, c : c + cols]).astype(types[n])

    return in_vmem(
        *pl.pallas_call(
            kernel,
            in_specs=[VMEM] * (2 + count),
            out_specs=[VMEM] * count,
            out_shape=[pltpu.VMEM((rows, width), t) for t in types],
            scratch_shapes=[pltpu.VMEM((rows, depth), BF)],
            compiler_params=params(5 * MIB),
            cost_estimate=cost(2 * rows * depth * width * count, 2 * rows * (depth + width)),
        )(*pieces, *weights)
    )


def natural_units(me):
    x, y, d = me ^ 1, me ^ 2, me ^ 3
    return [2 * me, 2 * me + 1, 2 * x + 1, 2 * y + 1, 2 * x, 2 * y, 2 * d, 2 * d + 1]


def known_state(me, groups, cum_columns, width):
    unit = groups[0][0].shape[0] // 2
    rows, heads = cum_columns.shape

    def kernel(me_ref, *refs):
        ks, vs, cum_ref = refs[0:3], refs[3:6], refs[6]
        s_out, left_out, left, keys, vals = refs[7:]
        total = cum_ref[rows - 1 : rows, :]
        for n, natural in enumerate(natural_units(me_ref[0])):
            cum = cum_ref[pl.ds(pl.multiple_of(natural * unit, unit), unit), :]
            left[n * unit : (n + 1) * unit, :] = jnp.exp(total - cum)
        left_out[...] = left[6 * unit :, :]
        for pair in range(heads // 2):
            here = slice(pair * 2 * HD, (pair + 1) * 2 * HD)
            for g in range(3):
                span = slice(2 * unit * g, 2 * unit * (g + 1))
                vals[span] = vs[g][:, here]
                for h in range(2):
                    lane = slice((2 * pair + h) * HD, (2 * pair + h + 1) * HD)
                    keys[span, h * HD : (h + 1) * HD] = (
                        ks[g][:, lane].astype(F32) * left[span, 2 * pair + h : 2 * pair + h + 1]
                    ).astype(BF)
            both = dot_dims(keys[...], vals[...], 0, 0)
            for h in range(2):
                s_out[(2 * pair + h) * HD : (2 * pair + h + 1) * HD] = both[
                    h * HD : (h + 1) * HD, h * HD : (h + 1) * HD
                ]

    return pl.pallas_call(
        kernel,
        in_specs=[SMEM] + [VMEM] * 7,
        out_specs=[VMEM] * 2,
        out_shape=[pltpu.VMEM((width, HD), F32), pltpu.VMEM((2 * unit, heads), F32)],
        scratch_shapes=[
            pltpu.VMEM((rows, heads), F32),
            pltpu.VMEM((6 * unit, 2 * HD), BF),
            pltpu.VMEM((6 * unit, 2 * HD), BF),
        ],
        compiler_params=params(4 * MIB),
        cost_estimate=cost(8 * rows * HD * width, 8 * rows * width),
    )(me, *[g[1] for g in groups], *[g[2] for g in groups], cum_columns)


def last_keys_and_state(pieces, w_k, w_v, known, left):
    unit, depth = pieces[0].shape
    rows, width, cols = 2 * unit, w_k.shape[1], 512
    here_heads = cols // HD

    def kernel(d0, d1, wk_ref, wv_ref, known_ref, left_ref, k_out, v_out, s_out, held, keys):
        held[:unit] = d0[...]
        held[unit:] = d1[...]
        for c in range(0, width, cols):
            k_part = dot(held[...], wk_ref[:, c : c + cols]).astype(BF)
            v_part = dot(held[...], wv_ref[:, c : c + cols]).astype(BF)
            k_out[:, c : c + cols] = k_part
            v_out[:, c : c + cols] = v_part
            first = c // HD
            for h in range(here_heads):
                keys[:, h * HD : (h + 1) * HD] = (
                    k_part[:, h * HD : (h + 1) * HD].astype(F32) * left_ref[:, first + h : first + h + 1]
                ).astype(BF)
            for pair in range(here_heads // 2):
                span = slice(pair * 2 * HD, (pair + 1) * 2 * HD)
                both = dot_dims(keys[:, span], v_part[:, span], 0, 0)
                for h in range(2):
                    head = slice((first + 2 * pair + h) * HD, (first + 2 * pair + h + 1) * HD)
                    s_out[head] = (known_ref[head] + both[h * HD : (h + 1) * HD, h * HD : (h + 1) * HD]).astype(BF)

    return pl.pallas_call(
        kernel,
        in_specs=[VMEM] * 6,
        out_specs=[VMEM] * 3,
        out_shape=[
            pltpu.VMEM((rows, width), BF),
            pltpu.VMEM((rows, width), BF),
            jax.ShapeDtypeStruct((width, HD), BF),
        ],
        scratch_shapes=[pltpu.VMEM((rows, depth), BF), pltpu.VMEM((rows, cols), BF)],
        compiler_params=params(5 * MIB),
        cost_estimate=cost(4 * rows * depth * width, 4 * rows * (depth + width)),
    )(*pieces, w_k, w_v, known, left)


def local_attention(me, groups, w_out, cum_columns, cum_rows, width):
    unit = groups[0][0].shape[0] // 2
    rows, heads = cum_columns.shape
    cols = 2 * HD
    blocks = rows // CH

    def kernel(me_ref, *refs):
        ins, (cc_ref, cr_ref, w_ref), outs, w_kept, done = refs[:12], refs[12:15], refs[15:23], refs[23], refs[24]
        q, k, v, a, s, w_sem = refs[25:]
        done[...] = jnp.zeros_like(done)
        w_copy = pltpu.make_async_copy(w_ref, w_kept, w_sem)
        w_copy.start()
        order = natural_units(me_ref[0])
        places = [pl.ds(pl.multiple_of(n * unit, unit), unit) for n in order]
        causal = lax.broadcasted_iota(jnp.int32, (CH, CH), 0) >= lax.broadcasted_iota(jnp.int32, (CH, CH), 1)
        lane = lax.broadcasted_iota(jnp.int32, (rows, heads), 1)
        sub = lax.broadcasted_iota(jnp.int32, (heads, rows), 0)

        def loop(pair, carry):
            lanes = pl.ds(pl.multiple_of(pair * cols, cols), cols)
            for kind, to in enumerate((q, k, v)):
                for n, place in enumerate(places):
                    at = (n % 2) * unit
                    to[place, :] = ins[3 * (n // 2) + kind][at : at + unit, lanes]
            for h in range(2):
                here = slice(h * HD, (h + 1) * HD)
                column = jnp.sum(jnp.where(lane == 2 * pair + h, cc_ref[...], 0.0), axis=1, keepdims=True)
                row = jnp.sum(jnp.where(sub == 2 * pair + h, cr_ref[...], 0.0), axis=0, keepdims=True)
                s[:, here] = (q[:, here].astype(F32) * jnp.exp(column)).astype(BF)
                state = jnp.zeros((HD, HD), F32)
                for b in range(blocks):
                    t = slice(b * CH, (b + 1) * CH)
                    qb, kb, vb = q[t, here], k[t, here], v[t, here]
                    ct, cs = column[t], row[:, t]
                    before = column[b * CH - 1 : b * CH] if b else jnp.zeros((1, 1), F32)
                    end = column[(b + 1) * CH - 1 : (b + 1) * CH]
                    weight = jnp.where(causal, jnp.exp(jnp.minimum(ct - cs, 0.0)), 0.0)
                    scores = (dot_dims(qb, kb, 1, 1) * weight).astype(BF)
                    within = dot(scores, vb)
                    if b:
                        within = within + dot(qb, state.astype(BF)) * jnp.exp(ct - before)
                    a[t, here] = within
                    if b < blocks - 1:
                        decayed = (kb.astype(F32) * jnp.exp(end - ct)).astype(BF)
                        state = jnp.exp(end - before) * state + dot_dims(decayed, vb, 0, 0)
            for n, place in enumerate(places):
                at = (n % 2) * unit
                outs[2 * (n // 2)][at : at + unit, lanes] = a[place, :]
                outs[2 * (n // 2) + 1][at : at + unit, lanes] = s[place, :]
            return carry

        lax.fori_loop(0, heads // 2, loop, 0)
        w_copy.wait()

    outs = pl.pallas_call(
        kernel,
        in_specs=[SMEM] + [VMEM] * 14 + [ANY],
        out_specs=[VMEM] * 10,
        out_shape=[pltpu.VMEM((2 * unit, width), t) for _ in range(4) for t in (F32, BF)]
        + [pltpu.VMEM(w_out.shape, BF), jax.ShapeDtypeStruct((8, HD), F32)],
        scratch_shapes=[pltpu.VMEM((rows, cols), BF)] * 3
        + [pltpu.VMEM((rows, cols), F32), pltpu.VMEM((rows, cols), BF), pltpu.SemaphoreType.DMA],
        compiler_params=params(SMALL),
        cost_estimate=cost(10 * rows * CH * width, 8 * rows * width),
    )(me, *[part for group in groups for part in group[:3]], cum_columns, cum_rows, w_out)
    *kept, done = outs
    kept = in_vmem(*kept)
    return [kept[2 * g : 2 * g + 2] for g in range(4)], kept[8], done


def decay_sums(decay_log):
    heads, rows = decay_log.shape

    def kernel(d_ref, rows_ref, columns_ref, total_ref):
        earlier = lax.broadcasted_iota(jnp.int32, (CH, CH), 0) <= lax.broadcasted_iota(jnp.int32, (CH, CH), 1)
        ones = jnp.where(earlier, 1.0, 0.0)
        ahead = jnp.zeros((heads, 1), F32)
        for b in range(rows // CH):
            here = slice(b * CH, (b + 1) * CH)
            sums = ahead + jnp.dot(
                d_ref[:, here], ones, preferred_element_type=F32, precision=lax.Precision.HIGHEST
            )
            rows_ref[:, here] = sums
            columns_ref[here, :] = sums.T
            ahead = sums[:, CH - 1 :]
        total_ref[...] = jnp.broadcast_to(ahead, (heads, HD))

    return pl.pallas_call(
        kernel,
        in_specs=[VMEM],
        out_specs=[VMEM] * 3,
        out_shape=[jax.ShapeDtypeStruct(shape, F32) for shape in ((heads, rows), (rows, heads), (heads, HD))],
        compiler_params=params(SMALL),
        cost_estimate=cost(12 * heads * rows * CH, 12 * heads * rows),
    )(decay_log)


def combined(core, pick, terms, factors, rows, after=()):
    heads = rows // HD

    def kernel(core_ref, *refs):
        ins, f_ref, out_ref = refs[: len(terms)], refs[len(terms)], refs[-1]
        for h in range(heads):
            total = None
            for n, ref in enumerate(ins):
                at = pick(n, core_ref[0], h) * HD
                term = ref[pl.ds(pl.multiple_of(at, HD), HD)].astype(F32) * f_ref[n, h : h + 1, :]
                total = term if total is None else total + term
            out_ref[h * HD : (h + 1) * HD] = total.astype(BF)

    return pl.pallas_call(
        kernel,
        in_specs=[SMEM] + [VMEM] * (len(terms) + 1) + [ANY] * len(after),
        out_specs=VMEM,
        out_shape=jax.ShapeDtypeStruct((rows, HD), BF),
        compiler_params=params(3 * MIB),
        cost_estimate=cost(2 * len(terms) * rows * HD, 2 * (len(terms) + 1) * rows * HD),
    )(core, *terms, factors, *after)


def state_factors(total):
    chips = lax.axis_size("seq") // 2
    rank = lax.axis_index("seq")
    core, chip = rank % 2, rank // 2
    heads = total.shape[0]
    half = heads // 2
    first = core == 0
    other = swapped(total, "seq", 1)
    own_half = lambda value: lax.dynamic_slice_in_dim(value, core * half, half, 0)
    one = jnp.ones((half, HD), F32)
    later = jnp.exp(own_half(jnp.where(first, other, total)))
    joining = jnp.stack([jnp.where(first, later, one), jnp.where(first, one, later)])
    chip_total = own_half(total + other)
    weights = []
    passed = jnp.zeros((half, HD), F32)
    for d in range(1, chips):
        weights.append(jnp.where(chip >= d, jnp.exp(passed), 0.0))
        if d < chips - 1:
            passed = passed + passed_along(chip_total, "seq", 2 * d)
    nothing = jnp.zeros((heads, HD), F32)
    decay = jnp.where(first, 1.0, jnp.exp(other))
    final = jnp.stack(
        [
            jnp.where(first, jnp.concatenate([decay[:half], nothing[half:]]), jnp.concatenate([nothing[:half], decay[half:]])),
            jnp.where(first, jnp.concatenate([nothing[:half], decay[half:]]), jnp.concatenate([decay[:half], nothing[half:]])),
            jnp.where(first, nothing, 1.0),
        ]
    )
    return joining, jnp.stack(weights), final


def state_of_chip(core, state, other, joining):
    half = state.shape[0] // 2
    heads = half // HD
    return combined(core, lambda n, c, h: c * heads + h, [state, other], joining, half)


def entering_state(core, chip_states, other, weights, final, after):
    half = chip_states[0].shape[0]
    heads = half // HD
    entering = combined(core, lambda n, c, h: h, chip_states, weights, half, [after])
    entering_other = swapped(entering, "seq", 1)
    return combined(
        core, lambda n, c, h: h if n == 2 else h % heads, [entering, entering_other, other], final, 2 * half
    )


def output_terms(parts, gain, incoming, w_out):
    unit = parts[0][0].shape[0] // 2
    width, model = w_out.shape
    cols = model // 4
    heads = width // HD

    def kernel(a0, s0, z0, a1, s1, z1, gain_ref, in_ref, w_ref, out_a, out_b, gated, kept, out_sems):
        for n, (a, s, z) in enumerate(((a0, s0, z0), (a1, s1, z1))):
            span = slice(parts[n][3] * unit, (parts[n][3] + 1) * unit)
            for h in range(heads):
                here = slice(h * HD, (h + 1) * HD)
                attended = a[span, here] + dot(s[span, here], in_ref[here])
                mean = jnp.mean(attended * attended, axis=1, keepdims=True)
                gate = z[span, here]
                gated[n * unit : (n + 1) * unit, here] = (
                    attended * lax.rsqrt(mean + EPSILON) * gain_ref[:, here] * (gate / (1.0 + jnp.exp(-gate)))
                ).astype(BF)
        outs = []
        for n in range(4):
            kept[n] = dot(gated[...], w_ref[:, n * cols : (n + 1) * cols]).astype(BF)
            target = out_a if n < 2 else out_b
            outs.append(pltpu.make_async_copy(kept.at[n], target.at[:, pl.ds((n % 2) * cols, cols)], out_sems.at[n]))
            outs[n].start()
        for copy in outs:
            copy.wait()

    args = [array for part in parts for array in part[:3]]
    return pl.pallas_call(
        kernel,
        in_specs=[VMEM] * 9,
        out_specs=[ANY] * 2,
        out_shape=[jax.ShapeDtypeStruct((2 * unit, model // 2), BF)] * 2,
        scratch_shapes=[
            pltpu.VMEM((2 * unit, width), BF),
            pltpu.VMEM((4, 2 * unit, cols), BF),
            pltpu.SemaphoreType.DMA((4,)),
        ],
        compiler_params=params(SMALL),
        cost_estimate=cost(4 * unit * width * model, 4 * unit * model),
    )(*args, gain, incoming, w_out)


def merged(own, arrived, widths, after):
    rows = own.shape[0]
    firsts = [sum(widths[:n]) for n in range(len(widths))]

    def kernel(a, b, after_ref, *outs):
        for first, width, out in zip(firsts, widths, outs):
            here = slice(first, first + width)
            out[...] = (a[:, here].astype(F32) + b[:, here].astype(F32)).astype(BF)

    return pl.pallas_call(
        kernel,
        in_specs=[VMEM] * 2 + [ANY],
        out_specs=[VMEM] * len(widths),
        out_shape=[jax.ShapeDtypeStruct((rows, width), BF) for width in widths],
        compiler_params=params(SMALL),
        cost_estimate=cost(rows * own.shape[1], 6 * rows * own.shape[1]),
    )(own, arrived, after)


def add_coarse(fine, columns, width, previous=None):
    rows, model = fine.shape
    pieces = 3
    tall = rows // pieces
    coarse = tall // SF
    flat = [term for _, terms in columns for term in terms]

    def kernel(fine_ref, *refs):
        terms, out_ref = refs[: len(flat)], refs[len(flat) + (previous is not None)]
        fine_buf, term_buf, kept, fine_sems, term_sems, out_sems = refs[-6:]
        term_copies, fine_copies, outs = [], [], []
        for n, (first, _) in enumerate(columns):
            for m in range(3):
                source = terms[3 * n + m].at[:, pl.ds(flat[3 * n + m][1], width)]
                copy = pltpu.make_async_copy(source, term_buf.at[3 * n + m], term_sems.at[3 * n + m])
                copy.start()
                term_copies.append(copy)
            for piece in range(pieces):
                place = (pl.ds(piece * tall, tall), pl.ds(first, width))
                at = pieces * n + piece
                copy = pltpu.make_async_copy(fine_ref.at[place], fine_buf.at[at], fine_sems.at[at])
                copy.start()
                fine_copies.append(copy)
                outs.append(pltpu.make_async_copy(kept.at[at], out_ref.at[place], out_sems.at[at]))
        r = lax.broadcasted_iota(jnp.int32, (tall, coarse), 0) // SF
        c = lax.broadcasted_iota(jnp.int32, (tall, coarse), 1)
        spread = jnp.where(r == c, 1.0, 0.0).astype(BF)
        for n in range(len(columns)):
            for m in range(3):
                term_copies[3 * n + m].wait()
            for piece in range(pieces):
                at = pieces * n + piece
                fine_copies[at].wait()
                total = fine_buf[at].astype(F32)
                for m in range(3):
                    total += dot(spread, term_buf[3 * n + m, piece * coarse : (piece + 1) * coarse])
                kept[at] = total.astype(BF)
                outs[at].start()
        for copy in outs:
            copy.wait()

    args = [fine] + [term for term, _ in flat]
    aliases = {}
    if previous is not None:
        args.append(previous)
        aliases = {len(args) - 1: 0}
    count = pieces * len(columns)
    return pl.pallas_call(
        kernel,
        in_specs=[ANY] * len(args),
        out_specs=ANY,
        out_shape=jax.ShapeDtypeStruct((rows, model), BF),
        input_output_aliases=aliases,
        scratch_shapes=[
            pltpu.VMEM((count, tall, width), BF),
            pltpu.VMEM((len(flat), rows // SF, width), BF),
            pltpu.VMEM((count, tall, width), BF),
            pltpu.SemaphoreType.DMA((count,)),
            pltpu.SemaphoreType.DMA((len(flat),)),
            pltpu.SemaphoreType.DMA((count,)),
        ],
        compiler_params=params(24 * MIB),
        cost_estimate=cost(12 * rows * coarse * width, 8 * rows * width),
    )(*args)


def body_square(fine_rows, w_inputs, w_out, head_gain, decay_log):
    model = fine_rows.shape[1]
    fine_count = fine_rows.shape[0]
    heads, rows_coarse = decay_log.shape
    width = heads * HD
    place = jnp.reshape(lax.axis_index("mp"), (1,)).astype(jnp.int32)
    core = jnp.reshape(lax.axis_index("seq") % 2, (1,)).astype(jnp.int32)

    before = passed_along(fine_rows[fine_count - 16 :], ("seq", "mp"), 1)
    p1 = pool_half(fine_rows, fine_rows, fine_count // 2, fine_count // 2 - 16)
    x1 = swapped(p1, "mp", 1)
    y1 = swapped(p1, "mp", 2)
    p0 = pool_half(fine_rows, before, 0, 0)
    x0 = swapped(p0, "mp", 1)
    y0 = swapped(p0, "mp", 2)
    cum_rows, cum_columns, total = decay_sums(decay_log)
    joining, state_weights, final = state_factors(total)
    w_q, w_k, w_v, w_g = weights = in_vmem(*prepare(w_inputs, p0, joining, state_weights, final))
    d1 = swapped(y1, "mp", 1)
    d0 = swapped(x0, "mp", 2)

    types = [BF, BF, BF, F32]
    first = project([p0, p1], weights, types)
    second = project([x1, y1], weights, types)
    third = project([x0, y0], weights, types)
    known, left = in_vmem(*known_state(place, [first, second, third], cum_columns, width))
    k_last, v_last, state = last_keys_and_state([d0, d1], w_k, w_v, known, left)
    k_last, v_last = in_vmem(k_last, v_last)
    other = swapped(state, "seq", 1)
    q_last, g_last = project([d0, d1], [w_q, w_g], [BF, F32])
    chip_state = state_of_chip(core, state, other, joining)
    chip_states = [passed_along(chip_state, "seq", 2 * d) for d in range(1, lax.axis_size("seq") // 2)]
    groups, w_kept, attended = local_attention(
        place, [first, second, third, [q_last, k_last, v_last]], pltpu.with_memory_space_constraint(w_out, pltpu.HBM), cum_columns, cum_rows, width
    )
    own, second, third, last = [(*group, gate) for group, gate in zip(groups, (first[3], second[3], third[3], g_last))]
    incoming = entering_state(core, chip_states, other, state_weights, final, attended)

    gain = head_gain[None]
    terms = lambda parts: output_terms(parts, gain, incoming, w_kept)
    far_a, far_b = terms([(*last, 0), (*last, 1)])
    got_a = swapped(far_a, "mp", 1)
    got_b = swapped(far_b, "mp", 2)
    x_a, x_b = terms([(*third, 0), (*second, 0)])
    from_x_a = swapped(x_a, "mp", 1)
    y_a, y_b = terms([(*third, 1), (*second, 1)])
    from_y_b = swapped(y_b, "mp", 2)
    own_a, own_b = terms([(*own, 0), (*own, 1)])
    half = model // 2
    widths = (half - half // 4, half // 4)
    from_x_b = [swapped(part, "mp", 1) for part in merged(x_b, got_b, widths, own_a)]
    from_y_a = [swapped(part, "mp", 2) for part in merged(y_a, got_a, widths, own_a)]
    out = None
    for n, at in enumerate((0, widths[0])):
        out = add_coarse(
            fine_rows,
            [
                (at, [(own_a, at), (from_x_a, at), (from_y_a[n], 0)]),
                (half + at, [(own_b, at), (from_y_b, at), (from_x_b[n], 0)]),
            ],
            widths[n],
            out,
        )
    return out


def body(fine_rows, w_inputs, w_out, head_gain, decay_log):
    model_width = fine_rows.shape[1]
    head_dim = D // ATTENDER_NUMBER
    local_heads = decay_log.shape[0]
    local_width = local_heads * head_dim
    rows_coarse = decay_log.shape[1]
    blocks = rows_coarse // CH
    fine_count = fine_rows.shape[0]
    tail_rows = fine_rows[fine_count - (SF - 1) :]
    before = passed_along(tail_rows, ("seq", "mp"), 1)
    widened = jnp.concatenate([before, fine_rows[: fine_count - (SF - 1)]], axis=0).astype(
        jnp.float32
    )
    pooled = jnp.mean(widened.reshape(-1, SF, model_width), axis=1).astype(jnp.bfloat16)
    weights_flat = w_inputs.reshape(model_width, 4 * local_width)
    projected = jnp.dot(
        lax.all_gather(pooled, "mp", axis=0, tiled=True),
        weights_flat,
        preferred_element_type=jnp.float32,
    )
    queries = (
        projected[:, :local_width].astype(jnp.bfloat16).reshape(blocks, CH, local_heads, head_dim)
    )
    key_rows = (
        projected[:, local_width : 2 * local_width]
        .astype(jnp.bfloat16)
        .reshape(blocks, CH, local_heads, head_dim)
    )
    values = (
        projected[:, 2 * local_width : 3 * local_width]
        .astype(jnp.bfloat16)
        .reshape(blocks, CH, local_heads, head_dim)
    )
    gate_values = projected[:, 3 * local_width :]
    cumulative = jnp.cumsum(decay_log.reshape(local_heads, blocks, CH), axis=2)
    gaps = cumulative[:, :, :, None] - cumulative[:, :, None, :]
    causal = jnp.arange(CH)[:, None] >= jnp.arange(CH)[None, :]
    weight = jnp.where(causal, jnp.exp(jnp.minimum(gaps, 0.0)), 0.0)
    scores = jnp.einsum("cthd,cshd->hcts", queries, key_rows, preferred_element_type=jnp.float32)
    scores = (scores * weight).astype(jnp.bfloat16)
    within = jnp.einsum("hcts,cshd->cthd", scores, values, preferred_element_type=jnp.float32)
    remaining = jnp.exp(cumulative[:, :, -1:] - cumulative)
    decayed_keys = (
        key_rows.astype(jnp.float32) * jnp.transpose(remaining, (1, 2, 0))[..., None]
    ).astype(jnp.bfloat16)
    block_states = jnp.einsum(
        "cshd,cshe->chde", decayed_keys, values, preferred_element_type=jnp.float32
    )
    block_decay = cumulative[:, :, -1]
    prefix_states = []
    prefix_decay = []
    running = jnp.zeros((local_heads, head_dim, head_dim), jnp.float32)
    decay_total = jnp.zeros((local_heads,), jnp.float32)
    for block_index in range(blocks):
        prefix_states.append(running)
        prefix_decay.append(decay_total)
        running = (
            jnp.exp(block_decay[:, block_index])[:, None, None] * running
            + block_states[block_index]
        )
        decay_total = decay_total + block_decay[:, block_index]
    shard_totals = lax.all_gather(decay_total[None, :], "seq", axis=0, tiled=True)
    my_rank = lax.axis_index("seq")
    running_ends = jnp.cumsum(shard_totals, axis=0)
    before_mine = lax.dynamic_slice_in_dim(running_ends - shard_totals, my_rank, 1, 0)
    shard_states = lax.all_gather(
        running[None].astype(jnp.bfloat16), "seq", axis=0, tiled=True
    ).astype(jnp.float32)
    row_count = shard_states.shape[0]
    span_sums = before_mine - running_ends
    device_rank = jnp.arange(row_count, dtype=jnp.int32)
    factor = jnp.where((device_rank < my_rank)[:, None], jnp.exp(jnp.minimum(span_sums, 0.0)), 0.0)
    incoming = jnp.zeros_like(running) + jnp.sum(factor[:, :, None, None] * shard_states, axis=0)
    entering = jnp.stack(
        [
            jnp.exp(prefix_decay[block_index])[:, None, None] * incoming
            + prefix_states[block_index]
            for block_index in range(blocks)
        ]
    )
    carried = jnp.einsum(
        "cthd,chde->cthe",
        queries,
        entering.astype(jnp.bfloat16),
        preferred_element_type=jnp.float32,
    )
    carried = carried * jnp.transpose(jnp.exp(cumulative), (1, 2, 0))[..., None]
    attended = (within + carried).reshape(rows_coarse, local_heads, head_dim)
    square_mean = jnp.mean(attended * attended, axis=2, keepdims=True)
    normed = (attended * lax.rsqrt(square_mean + EPSILON)).reshape(rows_coarse, local_width)
    gated_rows = (normed * head_gain * jax.nn.silu(gate_values)).astype(jnp.bfloat16)
    coarse = lax.psum_scatter(
        jnp.dot(gated_rows, w_out, preferred_element_type=jnp.float32).astype(jnp.bfloat16),
        "mp",
        scatter_dimension=0,
        tiled=True,
    ).astype(jnp.float32)
    upsampled = jnp.repeat(coarse, SF, axis=0)
    return (fine_rows.astype(jnp.float32) + upsampled).astype(jnp.bfloat16)


def solution(mesh):
    square = mesh.shape["mp"] == 4 and mesh.shape["seq"] % 2 == 0 and mesh.shape["seq"] > 2
    return jax.shard_map(
        body_square if square else body,
        mesh=mesh,
        in_specs=(
            P(("seq", "mp"), None),
            P(None, None, "mp"),
            P("mp", None),
            P("mp"),
            P("mp", "seq"),
        ),
        out_specs=P(("seq", "mp"), None),
        check_vma=False,
    )
```

```python
import jax
import jax.numpy as jnp
from jax import lax
from jax.experimental import pallas as pl
from jax.experimental.pallas import tpu as pltpu
from jax.sharding import PartitionSpec as P

D = 4096
ATTENDER_NUMBER = 32
SF = 4
CH = 128
HD = D // ATTENDER_NUMBER


EPSILON = 1e-05
BF = jnp.bfloat16
F32 = jnp.float32
MIB = 2**20
SMALL = 14 * MIB
ANY = pl.BlockSpec(memory_space=pl.ANY)
VMEM = pl.BlockSpec(memory_space=pltpu.VMEM)
SMEM = pl.BlockSpec(memory_space=pltpu.SMEM)


def passed_along(value, axis, by):
    peers = lax.axis_size(axis)
    pairs = [(i, i + by) for i in range(peers) if 0 <= i + by < peers]
    return lax.ppermute(value, axis, pairs)


def swapped(value, axis, bit):
    peers = lax.axis_size(axis)
    return lax.ppermute(value, axis, [(i, i ^ bit) for i in range(peers)])


def params(limit):
    return pltpu.CompilerParams(vmem_limit_bytes=limit)


def in_vmem(*arrays):
    return [pltpu.with_memory_space_constraint(array, pltpu.VMEM) for array in arrays]


def cost(flops, size):
    return pl.CostEstimate(flops=int(flops), bytes_accessed=int(size), transcendentals=0)


def dot(a, b):
    return jnp.dot(a, b, preferred_element_type=F32)


def dot_dims(a, b, da, db):
    return lax.dot_general(a, b, (((da,), (db,)), ((), ())), preferred_element_type=F32)


def pool(fine, before):
    rows, width = fine.shape[0] // 2, fine.shape[1]
    out_rows, parts = rows // SF, 4
    cols = width // parts
    jobs = [(half, n) for half in (1, 0) for n in range(parts)]

    def kernel(before_ref, fine_ref, low_ref, high_ref, ahead_rows, main_rows, pooled, before_sem, fine_sems, out_sems):
        before_copy = pltpu.make_async_copy(before_ref, ahead_rows, before_sem)
        copies = []
        for half, n in jobs:
            c = pl.ds(n * cols, cols)
            copies.append(
                pltpu.make_async_copy(
                    fine_ref.at[pl.ds(half * rows, rows), c],
                    main_rows.at[pl.ds(half * rows, rows), c],
                    fine_sems.at[half * parts + n],
                )
            )
            copies[-1].start()
        before_copy.start()
        j = lax.broadcasted_iota(jnp.int32, (out_rows, rows), 0) * SF
        i = lax.broadcasted_iota(jnp.int32, (out_rows, rows), 1)
        main = jnp.where((i <= j) & (i > j - SF), 1.0 / SF, 0.0).astype(BF)
        jt = lax.broadcasted_iota(jnp.int32, (out_rows, 16), 0) * SF
        it = lax.broadcasted_iota(jnp.int32, (out_rows, 16), 1) - 16
        ahead = jnp.where((it <= jt) & (it > jt - SF), 1.0 / SF, 0.0).astype(BF)
        outs = []
        for job, (half, n) in enumerate(jobs):
            c = slice(n * cols, (n + 1) * cols)
            if half == 1:
                copies[job].wait()
                copies[parts + n].wait()
            elif n == 0:
                before_copy.wait()
            tail = main_rows[rows - 16 : rows, c] if half == 1 else ahead_rows[:, c]
            total = dot(main, main_rows[half * rows : (half + 1) * rows, c]) + dot(ahead, tail)
            pooled[half, :, c] = total.astype(BF)
            target = high_ref if half == 1 else low_ref
            outs.append(
                pltpu.make_async_copy(pooled.at[half, :, pl.ds(n * cols, cols)], target.at[:, pl.ds(n * cols, cols)], out_sems.at[half * parts + n])
            )
            outs[-1].start()
        for copy in outs:
            copy.wait()

    return pl.pallas_call(
        kernel,
        in_specs=[ANY, ANY],
        out_specs=[ANY, ANY],
        out_shape=[jax.ShapeDtypeStruct((out_rows, width), BF)] * 2,
        scratch_shapes=[
            pltpu.VMEM((16, width), BF),
            pltpu.VMEM((2 * rows, width), BF),
            pltpu.VMEM((2, out_rows, width), BF),
            pltpu.SemaphoreType.DMA,
            pltpu.SemaphoreType.DMA((2 * parts,)),
            pltpu.SemaphoreType.DMA((2 * parts,)),
        ],
        compiler_params=params(58 * MIB),
        cost_estimate=cost(4 * out_rows * rows * width, 4 * rows * width),
    )(before, fine)


def held_back(array, after):
    def kernel(array_ref, after_ref, out_ref):
        pass

    return pl.pallas_call(
        kernel,
        in_specs=[ANY, ANY],
        out_specs=ANY,
        out_shape=jax.ShapeDtypeStruct(array.shape, array.dtype),
        input_output_aliases={0: 0},
        compiler_params=params(MIB),
        cost_estimate=cost(1, 1),
    )(array, after)


def prepare(raw, part, parts, *after):
    depth, kinds, width = raw.shape
    lanes = 128
    tiles = width // lanes
    per = kinds * tiles // parts
    group = 256 // per
    rows = raw.reshape(depth, kinds, tiles, lanes).transpose(0, 2, 1, 3).reshape(depth, parts * per, lanes)
    bk, slots, wide = 256, 4, 4
    steps = depth // bk

    def kernel(raw_ref, *refs):
        w_refs, (buf, sems) = refs[-2 - kinds : -2], refs[-2:]

        def fetch(step, slot):
            return pltpu.make_async_copy(
                raw_ref.at[pl.ds(pl.multiple_of(step * bk, bk), bk), pl.ds(part * per, per)], buf.at[slot], sems.at[slot]
            )

        for n in range(slots):
            fetch(n, n).start()
        to = lax.broadcasted_iota(jnp.int32, (256, 256), 0)
        of = lax.broadcasted_iota(jnp.int32, (256, 256), 1)
        order = jnp.where(of == (to % group) * per + to // group, 1.0, 0.0).astype(BF)

        def loop(step, carry):
            slot = lax.rem(step, slots)
            fetch(step, slot).wait()

            def some(i, carry):
                start = pl.multiple_of(i * wide * group, wide * group)
                blocks = [buf[slot, pl.ds(start + u * group, group)].reshape(256, lanes) for u in range(wide)]
                moved = dot(order, jnp.concatenate(blocks, axis=1))
                first = pl.multiple_of(step * bk + i * wide * group, wide * group)
                for u in range(wide):
                    for q in range(per):
                        w_refs[q % kinds][pl.ds(first + u * group, group), (q // kinds) * lanes : (q // kinds + 1) * lanes] = (
                            moved[q * group : (q + 1) * group, u * lanes : (u + 1) * lanes].astype(BF)
                        )
                return carry

            lax.fori_loop(0, bk // (wide * group), some, 0, unroll=True)

            @pl.when(step + slots < steps)
            def _():
                fetch(step + slots, slot).start()

            return carry

        lax.fori_loop(0, steps, loop, 0)

    return in_vmem(
        *pl.pallas_call(
            kernel,
            in_specs=[ANY] * (1 + len(after)),
            out_specs=[VMEM] * kinds,
            out_shape=[pltpu.VMEM((depth, width // parts), BF)] * kinds,
            scratch_shapes=[pltpu.VMEM((slots, bk, per, lanes), BF), pltpu.SemaphoreType.DMA((slots,))],
            compiler_params=params(8 * MIB),
            cost_estimate=cost(2 * depth * kinds * width * 256 // parts, 4 * depth * kinds * width // parts),
        )(rows, *after)
    )


def project(pieces, weights, types, *after):
    unit, depth = pieces[0].shape
    rows, cols, parts = 2 * unit, weights[0][0].shape[1], len(weights[0])
    count, width = len(weights), parts * weights[0][0].shape[1]

    def kernel(d0, d1, *refs):
        w_refs, outs, held = refs[: count * parts], refs[-1 - count : -1], refs[-1]
        held[:unit] = d0[...]
        held[unit:] = d1[...]
        for n in range(count):
            for c in range(parts):
                here = slice(c * cols, (c + 1) * cols)
                outs[n][:, here] = dot(held[...], w_refs[n * parts + c][...]).astype(types[n])

    return in_vmem(
        *pl.pallas_call(
            kernel,
            in_specs=[VMEM] * (2 + count * parts) + [ANY] * len(after),
            out_specs=[VMEM] * count,
            out_shape=[pltpu.VMEM((rows, width), t) for t in types],
            scratch_shapes=[pltpu.VMEM((rows, depth), BF)],
            compiler_params=params(5 * MIB),
            cost_estimate=cost(2 * rows * depth * width * count, 2 * rows * (depth + width)),
        )(*pieces, *[part for array in weights for part in array], *after)
    )


def natural_units(me):
    x, y, d = me ^ 1, me ^ 2, me ^ 3
    return [2 * me, 2 * me + 1, 2 * x + 1, 2 * y + 1, 2 * x, 2 * y, 2 * d, 2 * d + 1]


def known_state(me, groups, cum_columns, width):
    unit = groups[0][0].shape[0] // 2
    rows, heads = cum_columns.shape

    def kernel(me_ref, *refs):
        ks, vs, cum_ref = refs[0:3], refs[3:6], refs[6]
        s_out, left_out, left, keys, vals = refs[7:]
        total = cum_ref[rows - 1 : rows, :]
        for n, natural in enumerate(natural_units(me_ref[0])):
            cum = cum_ref[pl.ds(pl.multiple_of(natural * unit, unit), unit), :]
            left[n * unit : (n + 1) * unit, :] = jnp.exp(total - cum)
        left_out[...] = left[6 * unit :, :]
        for pair in range(heads // 2):
            here = slice(pair * 2 * HD, (pair + 1) * 2 * HD)
            for g in range(3):
                span = slice(2 * unit * g, 2 * unit * (g + 1))
                vals[span] = vs[g][:, here]
                for h in range(2):
                    lane = slice((2 * pair + h) * HD, (2 * pair + h + 1) * HD)
                    keys[span, h * HD : (h + 1) * HD] = (
                        ks[g][:, lane].astype(F32) * left[span, 2 * pair + h : 2 * pair + h + 1]
                    ).astype(BF)
            both = dot_dims(keys[...], vals[...], 0, 0)
            for h in range(2):
                s_out[(2 * pair + h) * HD : (2 * pair + h + 1) * HD] = both[
                    h * HD : (h + 1) * HD, h * HD : (h + 1) * HD
                ]

    return pl.pallas_call(
        kernel,
        in_specs=[SMEM] + [VMEM] * 7,
        out_specs=[VMEM] * 2,
        out_shape=[pltpu.VMEM((width, HD), F32), pltpu.VMEM((2 * unit, heads), F32)],
        scratch_shapes=[
            pltpu.VMEM((rows, heads), F32),
            pltpu.VMEM((6 * unit, 2 * HD), BF),
            pltpu.VMEM((6 * unit, 2 * HD), BF),
        ],
        compiler_params=params(4 * MIB),
        cost_estimate=cost(8 * rows * HD * width, 8 * rows * width),
    )(me, *[g[1] for g in groups], *[g[2] for g in groups], cum_columns)


def last_keys_and_state(pieces, w_k, w_v, known, left, width):
    unit, depth = pieces[0].shape
    rows, cols, parts = 2 * unit, w_k[0].shape[1], len(w_k)
    here_heads = cols // HD

    def kernel(d0, d1, *refs):
        wk_refs, wv_refs, (known_ref, left_ref, k_out, v_out, s_out, held, keys) = (
            refs[:parts],
            refs[parts : 2 * parts],
            refs[2 * parts :],
        )
        held[:unit] = d0[...]
        held[unit:] = d1[...]
        for c in range(0, width, cols):
            k_part = dot(held[...], wk_refs[c // cols][...]).astype(BF)
            v_part = dot(held[...], wv_refs[c // cols][...]).astype(BF)
            k_out[:, c : c + cols] = k_part
            v_out[:, c : c + cols] = v_part
            first = c // HD
            for h in range(here_heads):
                keys[:, h * HD : (h + 1) * HD] = (
                    k_part[:, h * HD : (h + 1) * HD].astype(F32) * left_ref[:, first + h : first + h + 1]
                ).astype(BF)
            for pair in range(here_heads // 2):
                span = slice(pair * 2 * HD, (pair + 1) * 2 * HD)
                both = dot_dims(keys[:, span], v_part[:, span], 0, 0)
                for h in range(2):
                    head = slice((first + 2 * pair + h) * HD, (first + 2 * pair + h + 1) * HD)
                    s_out[head] = (known_ref[head] + both[h * HD : (h + 1) * HD, h * HD : (h + 1) * HD]).astype(BF)

    return pl.pallas_call(
        kernel,
        in_specs=[VMEM] * (4 + 2 * parts),
        out_specs=[VMEM] * 3,
        out_shape=[
            pltpu.VMEM((rows, width), BF),
            pltpu.VMEM((rows, width), BF),
            jax.ShapeDtypeStruct((width, HD), BF),
        ],
        scratch_shapes=[pltpu.VMEM((rows, depth), BF), pltpu.VMEM((rows, cols), BF)],
        compiler_params=params(5 * MIB),
        cost_estimate=cost(4 * rows * depth * width, 4 * rows * (depth + width)),
    )(*pieces, *w_k, *w_v, known, left)


def local_attention(me, groups, w_out, cum_columns, cum_rows, width):
    unit = groups[0][0].shape[0] // 2
    rows, heads = cum_columns.shape
    together = 4 if heads % 4 == 0 else 2
    cols = together * HD
    blocks = rows // CH

    def kernel(me_ref, *refs):
        ins, (cc_ref, cr_ref, w_ref), outs, w_kept, done = refs[:12], refs[12:15], refs[15:23], refs[23], refs[24]
        q, k, v, a, s, w_sem = refs[25:]
        done[...] = jnp.zeros_like(done)
        w_copy = pltpu.make_async_copy(w_ref, w_kept, w_sem)
        w_copy.start()
        order = natural_units(me_ref[0])
        places = [pl.ds(pl.multiple_of(n * unit, unit), unit) for n in order]
        causal = lax.broadcasted_iota(jnp.int32, (CH, CH), 0) >= lax.broadcasted_iota(jnp.int32, (CH, CH), 1)
        lane = lax.broadcasted_iota(jnp.int32, (rows, heads), 1)
        sub = lax.broadcasted_iota(jnp.int32, (heads, rows), 0)

        def loop(pair, carry):
            lanes = pl.ds(pl.multiple_of(pair * cols, cols), cols)
            for kind, to in enumerate((q, k, v)):
                for n, place in enumerate(places):
                    at = (n % 2) * unit
                    to[place, :] = ins[3 * (n // 2) + kind][at : at + unit, lanes]
            for h in range(together):
                here = slice(h * HD, (h + 1) * HD)
                column = jnp.sum(jnp.where(lane == together * pair + h, cc_ref[...], 0.0), axis=1, keepdims=True)
                row = jnp.sum(jnp.where(sub == together * pair + h, cr_ref[...], 0.0), axis=0, keepdims=True)
                s[:, here] = (q[:, here].astype(F32) * jnp.exp(column)).astype(BF)
                state = jnp.zeros((HD, HD), F32)
                for b in range(blocks):
                    t = slice(b * CH, (b + 1) * CH)
                    qb, kb, vb = q[t, here], k[t, here], v[t, here]
                    ct, cs = column[t], row[:, t]
                    before = column[b * CH - 1 : b * CH] if b else jnp.zeros((1, 1), F32)
                    end = column[(b + 1) * CH - 1 : (b + 1) * CH]
                    weight = jnp.where(causal, jnp.exp(jnp.minimum(ct - cs, 0.0)), 0.0)
                    scores = (dot_dims(qb, kb, 1, 1) * weight).astype(BF)
                    within = dot(scores, vb)
                    if b:
                        within = within + dot(qb, state.astype(BF)) * jnp.exp(ct - before)
                    a[t, here] = within
                    if b < blocks - 1:
                        decayed = (kb.astype(F32) * jnp.exp(end - ct)).astype(BF)
                        state = jnp.exp(end - before) * state + dot_dims(decayed, vb, 0, 0)
            for n, place in enumerate(places):
                at = (n % 2) * unit
                outs[2 * (n // 2)][at : at + unit, lanes] = a[place, :]
                outs[2 * (n // 2) + 1][at : at + unit, lanes] = s[place, :]
            return carry

        lax.fori_loop(0, heads // together, loop, 0)
        w_copy.wait()

    outs = pl.pallas_call(
        kernel,
        in_specs=[SMEM] + [VMEM] * 14 + [ANY],
        out_specs=[VMEM] * 10,
        out_shape=[pltpu.VMEM((2 * unit, width), t) for _ in range(4) for t in (F32, BF)]
        + [pltpu.VMEM(w_out.shape, BF), jax.ShapeDtypeStruct((8, HD), F32)],
        scratch_shapes=[pltpu.VMEM((rows, cols), BF)] * 3
        + [pltpu.VMEM((rows, cols), F32), pltpu.VMEM((rows, cols), BF), pltpu.SemaphoreType.DMA],
        compiler_params=params(SMALL),
        cost_estimate=cost(10 * rows * CH * width, 8 * rows * width),
    )(me, *[part for group in groups for part in group[:3]], cum_columns, cum_rows, w_out)
    *kept, done = outs
    kept = in_vmem(*kept)
    return [kept[2 * g : 2 * g + 2] for g in range(4)], kept[8], done


def decay_sums(decay_log, after):
    heads, rows = decay_log.shape

    def kernel(d_ref, after_ref, rows_ref, columns_ref, total_ref):
        earlier = lax.broadcasted_iota(jnp.int32, (CH, CH), 0) <= lax.broadcasted_iota(jnp.int32, (CH, CH), 1)
        ones = jnp.where(earlier, 1.0, 0.0)
        ahead = jnp.zeros((heads, 1), F32)
        for b in range(rows // CH):
            here = slice(b * CH, (b + 1) * CH)
            sums = ahead + jnp.dot(
                d_ref[:, here], ones, preferred_element_type=F32, precision=lax.Precision.HIGHEST
            )
            rows_ref[:, here] = sums
            columns_ref[here, :] = sums.T
            ahead = sums[:, CH - 1 :]
        total_ref[...] = jnp.broadcast_to(ahead, (heads, HD))

    return pl.pallas_call(
        kernel,
        in_specs=[VMEM, ANY],
        out_specs=[VMEM] * 3,
        out_shape=[jax.ShapeDtypeStruct(shape, F32) for shape in ((heads, rows), (rows, heads), (heads, HD))],
        compiler_params=params(SMALL),
        cost_estimate=cost(12 * heads * rows * CH, 12 * heads * rows),
    )(decay_log, after)


def combined(core, pick, terms, factors, rows, after=()):
    heads = rows // HD

    def kernel(core_ref, *refs):
        ins, f_ref, out_ref = refs[: len(terms)], refs[len(terms)], refs[-1]
        for h in range(heads):
            total = None
            for n, ref in enumerate(ins):
                at = pick(n, core_ref[0], h) * HD
                term = ref[pl.ds(pl.multiple_of(at, HD), HD)].astype(F32) * f_ref[n, h : h + 1, :]
                total = term if total is None else total + term
            out_ref[h * HD : (h + 1) * HD] = total.astype(BF)

    return pl.pallas_call(
        kernel,
        in_specs=[SMEM] + [VMEM] * (len(terms) + 1) + [ANY] * len(after),
        out_specs=VMEM,
        out_shape=jax.ShapeDtypeStruct((rows, HD), BF),
        compiler_params=params(3 * MIB),
        cost_estimate=cost(2 * len(terms) * rows * HD, 2 * (len(terms) + 1) * rows * HD),
    )(core, *terms, factors, *after)


def state_factors(total):
    chips = lax.axis_size("seq") // 2
    rank = lax.axis_index("seq")
    core, chip = rank % 2, rank // 2
    heads = total.shape[0]
    half = heads // 2
    first = core == 0
    other = swapped(total, "seq", 1)
    own_half = lambda value: lax.dynamic_slice_in_dim(value, core * half, half, 0)
    one = jnp.ones((half, HD), F32)
    later = jnp.exp(own_half(jnp.where(first, other, total)))
    joining = jnp.stack([jnp.where(first, later, one), jnp.where(first, one, later)])
    chip_total = own_half(total + other)
    weights = []
    passed = jnp.zeros((half, HD), F32)
    for d in range(1, chips):
        weights.append(jnp.where(chip >= d, jnp.exp(passed), 0.0))
        if d < chips - 1:
            passed = passed + passed_along(chip_total, "seq", 2 * d)
    nothing = jnp.zeros((heads, HD), F32)
    decay = jnp.where(first, 1.0, jnp.exp(other))
    final = jnp.stack(
        [
            jnp.where(first, jnp.concatenate([decay[:half], nothing[half:]]), jnp.concatenate([nothing[:half], decay[half:]])),
            jnp.where(first, jnp.concatenate([nothing[:half], decay[half:]]), jnp.concatenate([decay[:half], nothing[half:]])),
            jnp.where(first, nothing, 1.0),
        ]
    )
    return joining, jnp.stack(weights), final


def state_of_chip(core, state, other, joining):
    half = state.shape[0] // 2
    heads = half // HD
    return combined(core, lambda n, c, h: c * heads + h, [state, other], joining, half)


def entering_state(core, chip_states, other, weights, final, after):
    half = chip_states[0].shape[0]
    heads = half // HD
    entering = combined(core, lambda n, c, h: h, chip_states, weights, half, [after])
    entering_other = swapped(entering, "seq", 1)
    return combined(
        core, lambda n, c, h: h if n == 2 else h % heads, [entering, entering_other, other], final, 2 * half
    )


def output_terms(parts, gain, incoming, w_out):
    unit = parts[0][0].shape[0] // 2
    width, model = w_out.shape
    cols = model // 4
    heads = width // HD

    def kernel(a0, s0, z0, a1, s1, z1, gain_ref, in_ref, w_ref, out_a, out_b, gated, kept, out_sems):
        for n, (a, s, z) in enumerate(((a0, s0, z0), (a1, s1, z1))):
            span = slice(parts[n][3] * unit, (parts[n][3] + 1) * unit)
            for h in range(heads):
                here = slice(h * HD, (h + 1) * HD)
                attended = a[span, here] + dot(s[span, here], in_ref[here])
                mean = jnp.mean(attended * attended, axis=1, keepdims=True)
                gate = z[span, here]
                gated[n * unit : (n + 1) * unit, here] = (
                    attended * lax.rsqrt(mean + EPSILON) * gain_ref[:, here] * (gate / (1.0 + jnp.exp(-gate)))
                ).astype(BF)
        outs = []
        for n in range(4):
            kept[n] = dot(gated[...], w_ref[:, n * cols : (n + 1) * cols]).astype(BF)
            target = out_a if n < 2 else out_b
            outs.append(pltpu.make_async_copy(kept.at[n], target.at[:, pl.ds((n % 2) * cols, cols)], out_sems.at[n]))
            outs[n].start()
        for copy in outs:
            copy.wait()

    args = [array for part in parts for array in part[:3]]
    return pl.pallas_call(
        kernel,
        in_specs=[VMEM] * 9,
        out_specs=[ANY] * 2,
        out_shape=[jax.ShapeDtypeStruct((2 * unit, model // 2), BF)] * 2,
        scratch_shapes=[
            pltpu.VMEM((2 * unit, width), BF),
            pltpu.VMEM((4, 2 * unit, cols), BF),
            pltpu.SemaphoreType.DMA((4,)),
        ],
        compiler_params=params(SMALL),
        cost_estimate=cost(4 * unit * width * model, 4 * unit * model),
    )(*args, gain, incoming, w_out)


def merged(own, arrived, widths, after):
    rows = own.shape[0]
    firsts = [sum(widths[:n]) for n in range(len(widths))]

    def kernel(a, b, after_ref, *outs):
        for first, width, out in zip(firsts, widths, outs):
            here = slice(first, first + width)
            out[...] = (a[:, here].astype(F32) + b[:, here].astype(F32)).astype(BF)

    return pl.pallas_call(
        kernel,
        in_specs=[VMEM] * 2 + [ANY],
        out_specs=[VMEM] * len(widths),
        out_shape=[jax.ShapeDtypeStruct((rows, width), BF) for width in widths],
        compiler_params=params(SMALL),
        cost_estimate=cost(rows * own.shape[1], 6 * rows * own.shape[1]),
    )(own, arrived, after)


def add_coarse(fine, columns, width, previous=None):
    rows, model = fine.shape
    pieces = 3
    tall = rows // pieces
    coarse = tall // SF
    flat = [term for _, terms in columns for term in terms]

    def kernel(fine_ref, *refs):
        terms, out_ref = refs[: len(flat)], refs[len(flat) + (previous is not None)]
        fine_buf, term_buf, kept, fine_sems, term_sems, out_sems = refs[-6:]
        term_copies, fine_copies, outs = [], [], []
        for n, (first, _) in enumerate(columns):
            for m in range(3):
                source = terms[3 * n + m].at[:, pl.ds(flat[3 * n + m][1], width)]
                copy = pltpu.make_async_copy(source, term_buf.at[3 * n + m], term_sems.at[3 * n + m])
                copy.start()
                term_copies.append(copy)
            for piece in range(pieces):
                place = (pl.ds(piece * tall, tall), pl.ds(first, width))
                at = pieces * n + piece
                copy = pltpu.make_async_copy(fine_ref.at[place], fine_buf.at[at], fine_sems.at[at])
                copy.start()
                fine_copies.append(copy)
                outs.append(pltpu.make_async_copy(kept.at[at], out_ref.at[place], out_sems.at[at]))
        r = lax.broadcasted_iota(jnp.int32, (tall, 3 * coarse), 0) // SF
        c = lax.broadcasted_iota(jnp.int32, (tall, 3 * coarse), 1) % coarse
        spread = jnp.where(r == c, 1.0, 0.0).astype(BF)
        for n in range(len(columns)):
            for m in range(3):
                term_copies[3 * n + m].wait()
            for piece in range(pieces):
                at = pieces * n + piece
                here = slice(piece * coarse, (piece + 1) * coarse)
                added = dot(spread, jnp.concatenate([term_buf[3 * n + m, here] for m in range(3)], axis=0))
                fine_copies[at].wait()
                kept[at] = (fine_buf[at].astype(F32) + added).astype(BF)
                outs[at].start()
        for copy in outs:
            copy.wait()

    args = [fine] + [term for term, _ in flat]
    aliases = {}
    if previous is not None:
        args.append(previous)
        aliases = {len(args) - 1: 0}
    count = pieces * len(columns)
    return pl.pallas_call(
        kernel,
        in_specs=[ANY] * len(args),
        out_specs=ANY,
        out_shape=jax.ShapeDtypeStruct((rows, model), BF),
        input_output_aliases=aliases,
        scratch_shapes=[
            pltpu.VMEM((count, tall, width), BF),
            pltpu.VMEM((len(flat), rows // SF, width), BF),
            pltpu.VMEM((count, tall, width), BF),
            pltpu.SemaphoreType.DMA((count,)),
            pltpu.SemaphoreType.DMA((len(flat),)),
            pltpu.SemaphoreType.DMA((count,)),
        ],
        compiler_params=params(24 * MIB),
        cost_estimate=cost(12 * rows * coarse * width, 8 * rows * width),
    )(*args)


def body_square(fine_rows, w_inputs, w_out, head_gain, decay_log):
    model = fine_rows.shape[1]
    fine_count = fine_rows.shape[0]
    heads, rows_coarse = decay_log.shape
    width = heads * HD
    place = jnp.reshape(lax.axis_index("mp"), (1,)).astype(jnp.int32)
    core = jnp.reshape(lax.axis_index("seq") % 2, (1,)).astype(jnp.int32)

    before = passed_along(fine_rows[fine_count - 16 :], ("seq", "mp"), 1)
    p0, p1 = pool(fine_rows, before)
    x1 = swapped(p1, "mp", 1)
    y1 = swapped(p1, "mp", 2)
    x0 = swapped(p0, "mp", 1)
    y0 = swapped(p0, "mp", 2)
    cum_rows, cum_columns, total = decay_sums(decay_log, p0)
    joining, state_weights, final = state_factors(total)
    parts = 2
    weights = [prepare(w_inputs, 0, parts, p0, joining, state_weights, final)]
    for part in range(1, parts):
        weights.append(prepare(w_inputs, part, parts, p0))
    w_q, w_k, w_v, w_g = weights = list(zip(*weights))
    d1 = swapped(y1, "mp", 1)

    types = [BF, BF, BF, F32]
    first = project([p0, p1], weights, types, y1)
    x0 = held_back(x0, first[0])
    d0 = swapped(x0, "mp", 2)
    second = project([x1, y1], weights, types)
    third = project([x0, y0], weights, types)
    known, left = in_vmem(*known_state(place, [first, second, third], cum_columns, width))
    k_last, v_last, state = last_keys_and_state([d0, d1], w_k, w_v, known, left, width)
    k_last, v_last = in_vmem(k_last, v_last)
    other = swapped(state, "seq", 1)
    q_last, g_last = project([d0, d1], [w_q, w_g], [BF, F32])
    chip_state = state_of_chip(core, state, other, joining)
    chip_states = [passed_along(chip_state, "seq", 2 * d) for d in range(1, lax.axis_size("seq") // 2)]
    groups, w_kept, attended = local_attention(
        place, [first, second, third, [q_last, k_last, v_last]], pltpu.with_memory_space_constraint(w_out, pltpu.HBM), cum_columns, cum_rows, width
    )
    own, second, third, last = [(*group, gate) for group, gate in zip(groups, (first[3], second[3], third[3], g_last))]
    incoming = entering_state(core, chip_states, other, state_weights, final, attended)

    gain = head_gain[None]
    terms = lambda parts: output_terms(parts, gain, incoming, w_kept)
    far_a, far_b = terms([(*last, 0), (*last, 1)])
    got_a = swapped(far_a, "mp", 1)
    got_b = swapped(far_b, "mp", 2)
    x_a, x_b = terms([(*third, 0), (*second, 0)])
    from_x_a = swapped(x_a, "mp", 1)
    y_a, y_b = terms([(*third, 1), (*second, 1)])
    from_y_b = swapped(y_b, "mp", 2)
    own_a, own_b = terms([(*own, 0), (*own, 1)])
    half = model // 2
    widths = (half * 11 // 16, half * 5 // 16)
    from_x_b = [swapped(part, "mp", 1) for part in merged(x_b, got_b, widths, own_a)]
    from_y_a = [swapped(part, "mp", 2) for part in merged(y_a, got_a, widths, own_a)]
    out = None
    for n, at in enumerate((0, widths[0])):
        out = add_coarse(
            fine_rows,
            [
                (at, [(own_a, at), (from_x_a, at), (from_y_a[n], 0)]),
                (half + at, [(own_b, at), (from_y_b, at), (from_x_b[n], 0)]),
            ],
            widths[n],
            out,
        )
    return out


def body(fine_rows, w_inputs, w_out, head_gain, decay_log):
    model_width = fine_rows.shape[1]
    head_dim = D // ATTENDER_NUMBER
    local_heads = decay_log.shape[0]
    local_width = local_heads * head_dim
    rows_coarse = decay_log.shape[1]
    blocks = rows_coarse // CH
    fine_count = fine_rows.shape[0]
    tail_rows = fine_rows[fine_count - (SF - 1) :]
    before = passed_along(tail_rows, ("seq", "mp"), 1)
    widened = jnp.concatenate([before, fine_rows[: fine_count - (SF - 1)]], axis=0).astype(
        jnp.float32
    )
    pooled = jnp.mean(widened.reshape(-1, SF, model_width), axis=1).astype(jnp.bfloat16)
    weights_flat = w_inputs.reshape(model_width, 4 * local_width)
    projected = jnp.dot(
        lax.all_gather(pooled, "mp", axis=0, tiled=True),
        weights_flat,
        preferred_element_type=jnp.float32,
    )
    queries = (
        projected[:, :local_width].astype(jnp.bfloat16).reshape(blocks, CH, local_heads, head_dim)
    )
    key_rows = (
        projected[:, local_width : 2 * local_width]
        .astype(jnp.bfloat16)
        .reshape(blocks, CH, local_heads, head_dim)
    )
    values = (
        projected[:, 2 * local_width : 3 * local_width]
        .astype(jnp.bfloat16)
        .reshape(blocks, CH, local_heads, head_dim)
    )
    gate_values = projected[:, 3 * local_width :]
    cumulative = jnp.cumsum(decay_log.reshape(local_heads, blocks, CH), axis=2)
    gaps = cumulative[:, :, :, None] - cumulative[:, :, None, :]
    causal = jnp.arange(CH)[:, None] >= jnp.arange(CH)[None, :]
    weight = jnp.where(causal, jnp.exp(jnp.minimum(gaps, 0.0)), 0.0)
    scores = jnp.einsum("cthd,cshd->hcts", queries, key_rows, preferred_element_type=jnp.float32)
    scores = (scores * weight).astype(jnp.bfloat16)
    within = jnp.einsum("hcts,cshd->cthd", scores, values, preferred_element_type=jnp.float32)
    remaining = jnp.exp(cumulative[:, :, -1:] - cumulative)
    decayed_keys = (
        key_rows.astype(jnp.float32) * jnp.transpose(remaining, (1, 2, 0))[..., None]
    ).astype(jnp.bfloat16)
    block_states = jnp.einsum(
        "cshd,cshe->chde", decayed_keys, values, preferred_element_type=jnp.float32
    )
    block_decay = cumulative[:, :, -1]
    prefix_states = []
    prefix_decay = []
    running = jnp.zeros((local_heads, head_dim, head_dim), jnp.float32)
    decay_total = jnp.zeros((local_heads,), jnp.float32)
    for block_index in range(blocks):
        prefix_states.append(running)
        prefix_decay.append(decay_total)
        running = (
            jnp.exp(block_decay[:, block_index])[:, None, None] * running
            + block_states[block_index]
        )
        decay_total = decay_total + block_decay[:, block_index]
    shard_totals = lax.all_gather(decay_total[None, :], "seq", axis=0, tiled=True)
    my_rank = lax.axis_index("seq")
    running_ends = jnp.cumsum(shard_totals, axis=0)
    before_mine = lax.dynamic_slice_in_dim(running_ends - shard_totals, my_rank, 1, 0)
    shard_states = lax.all_gather(
        running[None].astype(jnp.bfloat16), "seq", axis=0, tiled=True
    ).astype(jnp.float32)
    row_count = shard_states.shape[0]
    span_sums = before_mine - running_ends
    device_rank = jnp.arange(row_count, dtype=jnp.int32)
    factor = jnp.where((device_rank < my_rank)[:, None], jnp.exp(jnp.minimum(span_sums, 0.0)), 0.0)
    incoming = jnp.zeros_like(running) + jnp.sum(factor[:, :, None, None] * shard_states, axis=0)
    entering = jnp.stack(
        [
            jnp.exp(prefix_decay[block_index])[:, None, None] * incoming
            + prefix_states[block_index]
            for block_index in range(blocks)
        ]
    )
    carried = jnp.einsum(
        "cthd,chde->cthe",
        queries,
        entering.astype(jnp.bfloat16),
        preferred_element_type=jnp.float32,
    )
    carried = carried * jnp.transpose(jnp.exp(cumulative), (1, 2, 0))[..., None]
    attended = (within + carried).reshape(rows_coarse, local_heads, head_dim)
    square_mean = jnp.mean(attended * attended, axis=2, keepdims=True)
    normed = (attended * lax.rsqrt(square_mean + EPSILON)).reshape(rows_coarse, local_width)
    gated_rows = (normed * head_gain * jax.nn.silu(gate_values)).astype(jnp.bfloat16)
    coarse = lax.psum_scatter(
        jnp.dot(gated_rows, w_out, preferred_element_type=jnp.float32).astype(jnp.bfloat16),
        "mp",
        scatter_dimension=0,
        tiled=True,
    ).astype(jnp.float32)
    upsampled = jnp.repeat(coarse, SF, axis=0)
    return (fine_rows.astype(jnp.float32) + upsampled).astype(jnp.bfloat16)


def solution(mesh):
    square = mesh.shape["mp"] == 4 and mesh.shape["seq"] % 2 == 0 and mesh.shape["seq"] > 2
    return jax.shard_map(
        body_square if square else body,
        mesh=mesh,
        in_specs=(
            P(("seq", "mp"), None),
            P(None, None, "mp"),
            P("mp", None),
            P("mp"),
            P("mp", "seq"),
        ),
        out_specs=P(("seq", "mp"), None),
        check_vma=False,
    )
```

```python
import jax
import jax.numpy as jnp
from jax import lax
from jax.experimental import pallas as pl
from jax.experimental.pallas import tpu as pltpu
from jax.sharding import PartitionSpec as P

D = 4096
ATTENDER_NUMBER = 32
SF = 4
CH = 128
HD = D // ATTENDER_NUMBER


EPSILON = 1e-05
BF = jnp.bfloat16
F32 = jnp.float32
MIB = 2**20
SMALL = 9 * MIB
ANY = pl.BlockSpec(memory_space=pl.ANY)
VMEM = pl.BlockSpec(memory_space=pltpu.VMEM)
SMEM = pl.BlockSpec(memory_space=pltpu.SMEM)


def passed_along(value, axis, by):
    peers = lax.axis_size(axis)
    pairs = [(i, i + by) for i in range(peers) if 0 <= i + by < peers]
    return lax.ppermute(value, axis, pairs)


def swapped(value, axis, bit):
    peers = lax.axis_size(axis)
    return lax.ppermute(value, axis, [(i, i ^ bit) for i in range(peers)])


def params(limit):
    return pltpu.CompilerParams(vmem_limit_bytes=limit)


def in_vmem(*arrays):
    return [pltpu.with_memory_space_constraint(array, pltpu.VMEM) for array in arrays]


def cost(flops, size):
    return pl.CostEstimate(flops=int(flops) * 4, bytes_accessed=int(size) * 4, transcendentals=0)


def dot(a, b):
    return jnp.dot(a, b, preferred_element_type=F32)


def dot_dims(a, b, da, db):
    return lax.dot_general(a, b, (((da,), (db,)), ((), ())), preferred_element_type=F32)


def pool(fine, before):
    rows, width = fine.shape[0] // 2, fine.shape[1]
    out_rows, parts = rows // SF, 4
    cols = width // parts
    jobs = [(half, n) for half in (1, 0) for n in range(parts)]

    def kernel(before_ref, fine_ref, low_ref, high_ref, ahead_rows, main_rows, pooled, before_sem, fine_sems, out_sems):
        before_copy = pltpu.make_async_copy(before_ref, ahead_rows, before_sem)
        copies = []
        for half, n in jobs:
            c = pl.ds(n * cols, cols)
            copies.append(
                pltpu.make_async_copy(
                    fine_ref.at[pl.ds(half * rows, rows), c],
                    main_rows.at[pl.ds(half * rows, rows), c],
                    fine_sems.at[half * parts + n],
                )
            )
            copies[-1].start()
        before_copy.start()
        j = lax.broadcasted_iota(jnp.int32, (out_rows, rows), 0) * SF
        i = lax.broadcasted_iota(jnp.int32, (out_rows, rows), 1)
        main = jnp.where((i <= j) & (i > j - SF), 1.0 / SF, 0.0).astype(BF)
        jt = lax.broadcasted_iota(jnp.int32, (out_rows, 16), 0) * SF
        it = lax.broadcasted_iota(jnp.int32, (out_rows, 16), 1) - 16
        ahead = jnp.where((it <= jt) & (it > jt - SF), 1.0 / SF, 0.0).astype(BF)
        outs = []
        for job, (half, n) in enumerate(jobs):
            c = slice(n * cols, (n + 1) * cols)
            if half == 1:
                copies[job].wait()
                copies[parts + n].wait()
            elif n == 0:
                before_copy.wait()
            tail = main_rows[rows - 16 : rows, c] if half == 1 else ahead_rows[:, c]
            total = dot(main, main_rows[half * rows : (half + 1) * rows, c]) + dot(ahead, tail)
            pooled[half, :, c] = total.astype(BF)
            target = high_ref if half == 1 else low_ref
            outs.append(
                pltpu.make_async_copy(pooled.at[half, :, pl.ds(n * cols, cols)], target.at[:, pl.ds(n * cols, cols)], out_sems.at[half * parts + n])
            )
            outs[-1].start()
        for copy in outs:
            copy.wait()

    return pl.pallas_call(
        kernel,
        in_specs=[ANY, ANY],
        out_specs=[ANY, ANY],
        out_shape=[jax.ShapeDtypeStruct((out_rows, width), BF)] * 2,
        scratch_shapes=[
            pltpu.VMEM((16, width), BF),
            pltpu.VMEM((2 * rows, width), BF),
            pltpu.VMEM((2, out_rows, width), BF),
            pltpu.SemaphoreType.DMA,
            pltpu.SemaphoreType.DMA((2 * parts,)),
            pltpu.SemaphoreType.DMA((2 * parts,)),
        ],
        compiler_params=params(58 * MIB),
        cost_estimate=cost(4 * out_rows * rows * width, 4 * rows * width),
    )(before, fine)


def held_back(array, after):
    def kernel(array_ref, after_ref, out_ref):
        pass

    return pl.pallas_call(
        kernel,
        in_specs=[ANY, ANY],
        out_specs=ANY,
        out_shape=jax.ShapeDtypeStruct(array.shape, array.dtype),
        input_output_aliases={0: 0},
        compiler_params=params(MIB),
        cost_estimate=cost(1, 1),
    )(array, after)


def prepare(raw, part, parts, *after):
    depth, kinds, width = raw.shape
    lanes = 128
    tiles = width // lanes
    per = kinds * tiles // parts
    group = 256 // per
    rows = raw.reshape(depth, kinds, tiles, lanes).transpose(0, 2, 1, 3).reshape(depth, parts * per, lanes)
    bk, slots, wide = 256, 4, 4
    steps = depth // bk

    def kernel(raw_ref, *refs):
        w_refs, (buf, sems) = refs[-2 - kinds : -2], refs[-2:]

        def fetch(step, slot):
            return pltpu.make_async_copy(
                raw_ref.at[pl.ds(pl.multiple_of(step * bk, bk), bk), pl.ds(part * per, per)], buf.at[slot], sems.at[slot]
            )

        for n in range(slots):
            fetch(n, n).start()
        to = lax.broadcasted_iota(jnp.int32, (256, 256), 0)
        of = lax.broadcasted_iota(jnp.int32, (256, 256), 1)
        order = jnp.where(of == (to % group) * per + to // group, 1.0, 0.0).astype(BF)

        def loop(step, carry):
            slot = lax.rem(step, slots)
            fetch(step, slot).wait()

            def some(i, carry):
                start = pl.multiple_of(i * wide * group, wide * group)
                blocks = [buf[slot, pl.ds(start + u * group, group)].reshape(256, lanes) for u in range(wide)]
                moved = dot(order, jnp.concatenate(blocks, axis=1))
                first = pl.multiple_of(step * bk + i * wide * group, wide * group)
                for u in range(wide):
                    for q in range(per):
                        w_refs[q % kinds][pl.ds(first + u * group, group), (q // kinds) * lanes : (q // kinds + 1) * lanes] = (
                            moved[q * group : (q + 1) * group, u * lanes : (u + 1) * lanes].astype(BF)
                        )
                return carry

            lax.fori_loop(0, bk // (wide * group), some, 0, unroll=True)

            @pl.when(step + slots < steps)
            def _():
                fetch(step + slots, slot).start()

            return carry

        lax.fori_loop(0, steps, loop, 0)

    return in_vmem(
        *pl.pallas_call(
            kernel,
            in_specs=[ANY] * (1 + len(after)),
            out_specs=[VMEM] * kinds,
            out_shape=[pltpu.VMEM((depth, width // parts), BF)] * kinds,
            scratch_shapes=[pltpu.VMEM((slots, bk, per, lanes), BF), pltpu.SemaphoreType.DMA((slots,))],
            compiler_params=params(8 * MIB),
            cost_estimate=cost(1, 1),
        )(rows, *after)
    )


def project(pieces, weights, types, *after):
    unit, depth = pieces[0].shape
    rows, cols, parts = 2 * unit, weights[0][0].shape[1], len(weights[0])
    count, width = len(weights), parts * weights[0][0].shape[1]

    def kernel(d0, d1, *refs):
        w_refs, outs, held = refs[: count * parts], refs[-1 - count : -1], refs[-1]
        held[:unit] = d0[...]
        held[unit:] = d1[...]
        for n in range(count):
            for c in range(parts):
                here = slice(c * cols, (c + 1) * cols)
                outs[n][:, here] = dot(held[...], w_refs[n * parts + c][...]).astype(types[n])

    return in_vmem(
        *pl.pallas_call(
            kernel,
            in_specs=[VMEM] * (2 + count * parts) + [ANY] * len(after),
            out_specs=[VMEM] * count,
            out_shape=[pltpu.VMEM((rows, width), t) for t in types],
            scratch_shapes=[pltpu.VMEM((rows, depth), BF)],
            compiler_params=params(5 * MIB),
            cost_estimate=cost(rows * depth * width * count // 2, rows * (depth + width) // 2),
        )(*pieces, *[part for array in weights for part in array], *after)
    )


def natural_units(me):
    x, y, d = me ^ 1, me ^ 2, me ^ 3
    return [2 * me, 2 * me + 1, 2 * x + 1, 2 * y + 1, 2 * x, 2 * y, 2 * d, 2 * d + 1]


def known_state(me, groups, cum_columns, width):
    unit = groups[0][0].shape[0] // 2
    rows, heads = cum_columns.shape

    def kernel(me_ref, *refs):
        ks, vs, cum_ref = refs[0:3], refs[3:6], refs[6]
        s_out, left_out, left, keys, vals = refs[7:]
        total = cum_ref[rows - 1 : rows, :]
        for n, natural in enumerate(natural_units(me_ref[0])):
            cum = cum_ref[pl.ds(pl.multiple_of(natural * unit, unit), unit), :]
            left[n * unit : (n + 1) * unit, :] = jnp.exp(total - cum)
        left_out[...] = left[6 * unit :, :]
        for pair in range(heads // 2):
            here = slice(pair * 2 * HD, (pair + 1) * 2 * HD)
            for g in range(3):
                span = slice(2 * unit * g, 2 * unit * (g + 1))
                vals[span] = vs[g][:, here]
                for h in range(2):
                    lane = slice((2 * pair + h) * HD, (2 * pair + h + 1) * HD)
                    keys[span, h * HD : (h + 1) * HD] = (
                        ks[g][:, lane].astype(F32) * left[span, 2 * pair + h : 2 * pair + h + 1]
                    ).astype(BF)
            both = dot_dims(keys[...], vals[...], 0, 0)
            for h in range(2):
                s_out[(2 * pair + h) * HD : (2 * pair + h + 1) * HD] = both[
                    h * HD : (h + 1) * HD, h * HD : (h + 1) * HD
                ]

    return pl.pallas_call(
        kernel,
        in_specs=[SMEM] + [VMEM] * 7,
        out_specs=[VMEM] * 2,
        out_shape=[pltpu.VMEM((width, HD), F32), pltpu.VMEM((2 * unit, heads), F32)],
        scratch_shapes=[
            pltpu.VMEM((rows, heads), F32),
            pltpu.VMEM((6 * unit, 2 * HD), BF),
            pltpu.VMEM((6 * unit, 2 * HD), BF),
        ],
        compiler_params=params(4 * MIB),
        cost_estimate=cost(8 * rows * HD * width, 8 * rows * width),
    )(me, *[g[1] for g in groups], *[g[2] for g in groups], cum_columns)


def last_keys_and_state(pieces, w_k, w_v, known, left, total, width):
    unit, depth = pieces[0].shape
    rows, cols, parts = 2 * unit, w_k[0].shape[1], len(w_k)
    here_heads = cols // HD

    def kernel(d0, d1, *refs):
        wk_refs, wv_refs, (known_ref, left_ref, total_ref, k_out, v_out, s_out, held, keys) = (
            refs[:parts],
            refs[parts : 2 * parts],
            refs[2 * parts :],
        )
        held[:unit] = d0[...]
        held[unit:] = d1[...]
        s_out[width:] = as_terms(total_ref[...])
        for c in range(0, width, cols):
            k_part = dot(held[...], wk_refs[c // cols][...]).astype(BF)
            v_part = dot(held[...], wv_refs[c // cols][...]).astype(BF)
            k_out[:, c : c + cols] = k_part
            v_out[:, c : c + cols] = v_part
            first = c // HD
            for h in range(here_heads):
                keys[:, h * HD : (h + 1) * HD] = (
                    k_part[:, h * HD : (h + 1) * HD].astype(F32) * left_ref[:, first + h : first + h + 1]
                ).astype(BF)
            for pair in range(here_heads // 2):
                span = slice(pair * 2 * HD, (pair + 1) * 2 * HD)
                both = dot_dims(keys[:, span], v_part[:, span], 0, 0)
                for h in range(2):
                    head = slice((first + 2 * pair + h) * HD, (first + 2 * pair + h + 1) * HD)
                    s_out[head] = (known_ref[head] + both[h * HD : (h + 1) * HD, h * HD : (h + 1) * HD]).astype(BF)

    return pl.pallas_call(
        kernel,
        in_specs=[VMEM] * (5 + 2 * parts),
        out_specs=[VMEM] * 3,
        out_shape=[
            pltpu.VMEM((rows, width), BF),
            pltpu.VMEM((rows, width), BF),
            jax.ShapeDtypeStruct((width // HD * (HD + 4), HD), BF),
        ],
        scratch_shapes=[pltpu.VMEM((rows, depth), BF), pltpu.VMEM((rows, cols), BF)],
        compiler_params=params(5 * MIB),
        cost_estimate=cost(4 * rows * depth * width, 4 * rows * (depth + width)),
    )(*pieces, *w_k, *w_v, known, left, total)


def local_attention(me, groups, w_out, cum_columns, cum_rows, width):
    unit = groups[0][0].shape[0] // 2
    rows, heads = cum_columns.shape
    together = 4 if heads % 4 == 0 else 2
    cols = together * HD
    blocks = rows // CH

    def kernel(me_ref, *refs):
        ins, (cc_ref, cr_ref, w_ref), outs, w_kept, done = refs[:12], refs[12:15], refs[15:23], refs[23], refs[24]
        q, k, v, a, s, w_sem = refs[25:]
        done[...] = jnp.zeros_like(done)
        w_copy = pltpu.make_async_copy(w_ref, w_kept, w_sem)
        w_copy.start()
        order = natural_units(me_ref[0])
        places = [pl.ds(pl.multiple_of(n * unit, unit), unit) for n in order]
        causal = lax.broadcasted_iota(jnp.int32, (CH, CH), 0) >= lax.broadcasted_iota(jnp.int32, (CH, CH), 1)
        lane = lax.broadcasted_iota(jnp.int32, (rows, heads), 1)
        sub = lax.broadcasted_iota(jnp.int32, (heads, rows), 0)

        def loop(pair, carry):
            lanes = pl.ds(pl.multiple_of(pair * cols, cols), cols)
            for kind, to in enumerate((q, k, v)):
                for n, place in enumerate(places):
                    at = (n % 2) * unit
                    to[place, :] = ins[3 * (n // 2) + kind][at : at + unit, lanes]
            for h in range(together):
                here = slice(h * HD, (h + 1) * HD)
                column = jnp.sum(jnp.where(lane == together * pair + h, cc_ref[...], 0.0), axis=1, keepdims=True)
                row = jnp.sum(jnp.where(sub == together * pair + h, cr_ref[...], 0.0), axis=0, keepdims=True)
                s[:, here] = (q[:, here].astype(F32) * jnp.exp(column)).astype(BF)
                state = jnp.zeros((HD, HD), F32)
                for b in range(blocks):
                    t = slice(b * CH, (b + 1) * CH)
                    qb, kb, vb = q[t, here], k[t, here], v[t, here]
                    ct, cs = column[t], row[:, t]
                    before = column[b * CH - 1 : b * CH] if b else jnp.zeros((1, 1), F32)
                    end = column[(b + 1) * CH - 1 : (b + 1) * CH]
                    weight = jnp.where(causal, jnp.exp(jnp.minimum(ct - cs, 0.0)), 0.0)
                    scores = (dot_dims(qb, kb, 1, 1) * weight).astype(BF)
                    within = dot(scores, vb)
                    if b:
                        within = within + dot(qb, state.astype(BF)) * jnp.exp(ct - before)
                    a[t, here] = within
                    if b < blocks - 1:
                        decayed = (kb.astype(F32) * jnp.exp(end - ct)).astype(BF)
                        state = jnp.exp(end - before) * state + dot_dims(decayed, vb, 0, 0)
            for n, place in enumerate(places):
                at = (n % 2) * unit
                outs[2 * (n // 2)][at : at + unit, lanes] = a[place, :]
                outs[2 * (n // 2) + 1][at : at + unit, lanes] = s[place, :]
            return carry

        lax.fori_loop(0, heads // together, loop, 0)
        w_copy.wait()

    outs = pl.pallas_call(
        kernel,
        in_specs=[SMEM] + [VMEM] * 14 + [ANY],
        out_specs=[VMEM] * 10,
        out_shape=[pltpu.VMEM((2 * unit, width), t) for _ in range(4) for t in (F32, BF)]
        + [pltpu.VMEM(w_out.shape, BF), jax.ShapeDtypeStruct((8, HD), F32)],
        scratch_shapes=[pltpu.VMEM((rows, cols), BF)] * 3
        + [pltpu.VMEM((rows, cols), F32), pltpu.VMEM((rows, cols), BF), pltpu.SemaphoreType.DMA],
        compiler_params=params(SMALL),
        cost_estimate=cost(10 * rows * CH * width, 8 * rows * width),
    )(me, *[part for group in groups for part in group[:3]], cum_columns, cum_rows, w_out)
    *kept, done = outs
    kept = in_vmem(*kept)
    return [kept[2 * g : 2 * g + 2] for g in range(4)], kept[8], done


def decay_sums(decay_log, after):
    heads, rows = decay_log.shape

    def kernel(d_ref, after_ref, rows_ref, columns_ref, total_ref):
        earlier = lax.broadcasted_iota(jnp.int32, (CH, CH), 0) <= lax.broadcasted_iota(jnp.int32, (CH, CH), 1)
        ones = jnp.where(earlier, 1.0, 0.0)
        ahead = jnp.zeros((heads, 1), F32)
        for b in range(rows // CH):
            here = slice(b * CH, (b + 1) * CH)
            sums = ahead + jnp.dot(
                d_ref[:, here], ones, preferred_element_type=F32, precision=lax.Precision.HIGHEST
            )
            rows_ref[:, here] = sums
            columns_ref[here, :] = sums.T
            ahead = sums[:, CH - 1 :]
        total_ref[...] = jnp.broadcast_to(ahead, (heads, HD))

    return pl.pallas_call(
        kernel,
        in_specs=[VMEM, ANY],
        out_specs=[VMEM] * 3,
        out_shape=[jax.ShapeDtypeStruct(shape, F32) for shape in ((heads, rows), (rows, heads), (heads, HD))],
        compiler_params=params(3 * MIB),
        cost_estimate=cost(12 * heads * rows * CH, 12 * heads * rows),
    )(decay_log, after)


def as_terms(decays):
    high = decays.astype(BF).astype(F32)
    middle = (decays - high).astype(BF).astype(F32)
    low = decays - high - middle
    return jnp.concatenate([high, middle, low, jnp.zeros_like(decays)], axis=0).astype(BF)


def from_terms(terms):
    heads = terms.shape[0] // 4
    terms = terms.astype(F32)
    return terms[:heads] + terms[heads : 2 * heads] + terms[2 * heads : 3 * heads]


def state_of_chip(core, state, other, total):
    heads = total.shape[0]
    half = heads // 2

    def kernel(core_ref, s_ref, o_ref, total_ref, out_ref):
        c = core_ref[0]
        second = c.astype(F32)
        pick = lambda low, high: (1.0 - second) * low + second * high
        mine, theirs = total_ref[...], from_terms(o_ref[heads * HD :])
        decay = jnp.exp(pick(theirs, mine))
        for_mine, for_theirs = pick(decay, jnp.ones_like(decay)), pick(jnp.ones_like(decay), decay)
        for h in range(half):
            rows = pl.ds(pl.multiple_of((c * half + h) * HD, HD), HD)
            a, b = (pick(x[h : h + 1], x[half + h : half + h + 1]) for x in (for_mine, for_theirs))
            out_ref[h * HD : (h + 1) * HD] = (s_ref[rows].astype(F32) * a + o_ref[rows].astype(F32) * b).astype(BF)
        both = mine + theirs
        out_ref[half * HD :] = as_terms(pick(both[:half], both[half:]))

    return pl.pallas_call(
        kernel,
        in_specs=[SMEM] + [VMEM] * 3,
        out_specs=VMEM,
        out_shape=jax.ShapeDtypeStruct((half * (HD + 4), HD), BF),
        compiler_params=params(3 * MIB),
        cost_estimate=cost(4 * half * HD * HD, 6 * half * HD * HD),
    )(core, state, other, total)


def entering_chip(chip_states, after):
    half = chip_states[0].shape[0] // (HD + 4)

    def kernel(*refs):
        ins, out_ref = refs[: len(chip_states)], refs[-1]
        passed = jnp.zeros((half, HD), F32)
        weights = []
        for ref in ins:
            weights.append(jnp.exp(passed))
            passed = passed + from_terms(ref[half * HD :])
        for h in range(half):
            rows = slice(h * HD, (h + 1) * HD)
            out_ref[rows] = sum(ref[rows].astype(F32) * w[h : h + 1] for ref, w in zip(ins, weights)).astype(BF)

    return pl.pallas_call(
        kernel,
        in_specs=[VMEM] * len(chip_states) + [ANY],
        out_specs=VMEM,
        out_shape=jax.ShapeDtypeStruct((half * HD, HD), BF),
        compiler_params=params(3 * MIB),
        cost_estimate=cost(6 * half * HD * HD, 8 * half * HD * HD),
    )(*chip_states, after)


def entering_shard(core, entering, entering_other, other):
    half = entering.shape[0] // HD
    heads = 2 * half

    def kernel(core_ref, mine_ref, theirs_ref, o_ref, out_ref):
        second = core_ref[0].astype(F32)
        decay = (1.0 - second) + second * jnp.exp(from_terms(o_ref[heads * HD :]))
        for h in range(heads):
            low, high = (mine_ref, theirs_ref) if h < half else (theirs_ref, mine_ref)
            rows, here = slice(h * HD, (h + 1) * HD), slice(h % half * HD, (h % half + 1) * HD)
            state = (1.0 - second) * low[here].astype(F32) + second * high[here].astype(F32)
            out_ref[rows] = (state * decay[h : h + 1] + second * o_ref[rows].astype(F32)).astype(BF)

    return pl.pallas_call(
        kernel,
        in_specs=[SMEM] + [VMEM] * 3,
        out_specs=VMEM,
        out_shape=jax.ShapeDtypeStruct((heads * HD, HD), BF),
        compiler_params=params(3 * MIB),
        cost_estimate=cost(4 * heads * HD * HD, 8 * heads * HD * HD),
    )(core, entering, entering_other, other)


def output_terms(parts, gain, incoming, w_out):
    unit = parts[0][0].shape[0] // 2
    width, model = w_out.shape
    cols = model // 4
    heads = width // HD

    def kernel(a0, s0, z0, a1, s1, z1, gain_ref, in_ref, w_ref, out_a, out_b, gated, kept, out_sems):
        for n, (a, s, z) in enumerate(((a0, s0, z0), (a1, s1, z1))):
            span = slice(parts[n][3] * unit, (parts[n][3] + 1) * unit)
            for h in range(heads):
                here = slice(h * HD, (h + 1) * HD)
                attended = a[span, here] + dot(s[span, here], in_ref[here])
                mean = jnp.mean(attended * attended, axis=1, keepdims=True)
                gate = z[span, here]
                gated[n * unit : (n + 1) * unit, here] = (
                    attended * lax.rsqrt(mean + EPSILON) * gain_ref[:, here] * (gate / (1.0 + jnp.exp(-gate)))
                ).astype(BF)
        outs = []
        for n in range(4):
            kept[n] = dot(gated[...], w_ref[:, n * cols : (n + 1) * cols]).astype(BF)
            target = out_a if n < 2 else out_b
            outs.append(pltpu.make_async_copy(kept.at[n], target.at[:, pl.ds((n % 2) * cols, cols)], out_sems.at[n]))
            outs[n].start()
        for copy in outs:
            copy.wait()

    args = [array for part in parts for array in part[:3]]
    return pl.pallas_call(
        kernel,
        in_specs=[VMEM] * 9,
        out_specs=[ANY] * 2,
        out_shape=[jax.ShapeDtypeStruct((2 * unit, model // 2), BF)] * 2,
        scratch_shapes=[
            pltpu.VMEM((2 * unit, width), BF),
            pltpu.VMEM((4, 2 * unit, cols), BF),
            pltpu.SemaphoreType.DMA((4,)),
        ],
        compiler_params=params(SMALL),
        cost_estimate=cost(4 * unit * width * model, 4 * unit * model),
    )(*args, gain, incoming, w_out)


def merged(own, arrived, widths, after):
    rows = own.shape[0]
    firsts = [sum(widths[:n]) for n in range(len(widths))]

    def kernel(a, b, after_ref, *outs):
        for first, width, out in zip(firsts, widths, outs):
            here = slice(first, first + width)
            out[...] = (a[:, here].astype(F32) + b[:, here].astype(F32)).astype(BF)

    return pl.pallas_call(
        kernel,
        in_specs=[VMEM] * 2 + [ANY],
        out_specs=[VMEM] * len(widths),
        out_shape=[jax.ShapeDtypeStruct((rows, width), BF) for width in widths],
        compiler_params=params(SMALL),
        cost_estimate=cost(rows * own.shape[1], 6 * rows * own.shape[1]),
    )(own, arrived, after)


def add_coarse(fine, columns, width, previous=None):
    rows, model = fine.shape
    pieces = 3
    tall = rows // pieces
    coarse = tall // SF
    flat = [term for _, terms in columns for term in terms]

    def kernel(fine_ref, *refs):
        terms, out_ref = refs[: len(flat)], refs[len(flat) + (previous is not None)]
        fine_buf, term_buf, kept, fine_sems, term_sems, out_sems = refs[-6:]
        term_copies, fine_copies, outs = [], [], []
        for n, (first, _) in enumerate(columns):
            for m in range(3):
                source = terms[3 * n + m].at[:, pl.ds(flat[3 * n + m][1], width)]
                copy = pltpu.make_async_copy(source, term_buf.at[3 * n + m], term_sems.at[3 * n + m])
                copy.start()
                term_copies.append(copy)
            for piece in range(pieces):
                place = (pl.ds(piece * tall, tall), pl.ds(first, width))
                at = pieces * n + piece
                copy = pltpu.make_async_copy(fine_ref.at[place], fine_buf.at[at], fine_sems.at[at])
                copy.start()
                fine_copies.append(copy)
                outs.append(pltpu.make_async_copy(kept.at[at], out_ref.at[place], out_sems.at[at]))
        r = lax.broadcasted_iota(jnp.int32, (tall, 3 * coarse), 0) // SF
        c = lax.broadcasted_iota(jnp.int32, (tall, 3 * coarse), 1) % coarse
        spread = jnp.where(r == c, 1.0, 0.0).astype(BF)
        for n in range(len(columns)):
            for m in range(3):
                term_copies[3 * n + m].wait()
            for piece in range(pieces):
                at = pieces * n + piece
                here = slice(piece * coarse, (piece + 1) * coarse)
                added = dot(spread, jnp.concatenate([term_buf[3 * n + m, here] for m in range(3)], axis=0))
                fine_copies[at].wait()
                kept[at] = (fine_buf[at].astype(F32) + added).astype(BF)
                outs[at].start()
        for copy in outs:
            copy.wait()

    args = [fine] + [term for term, _ in flat]
    aliases = {}
    if previous is not None:
        args.append(previous)
        aliases = {len(args) - 1: 0}
    count = pieces * len(columns)
    return pl.pallas_call(
        kernel,
        in_specs=[ANY] * len(args),
        out_specs=ANY,
        out_shape=jax.ShapeDtypeStruct((rows, model), BF),
        input_output_aliases=aliases,
        scratch_shapes=[
            pltpu.VMEM((count, tall, width), BF),
            pltpu.VMEM((len(flat), rows // SF, width), BF),
            pltpu.VMEM((count, tall, width), BF),
            pltpu.SemaphoreType.DMA((count,)),
            pltpu.SemaphoreType.DMA((len(flat),)),
            pltpu.SemaphoreType.DMA((count,)),
        ],
        compiler_params=params(24 * MIB),
        cost_estimate=cost(12 * rows * coarse * width, 8 * rows * width),
    )(*args)


def body_square(fine_rows, w_inputs, w_out, head_gain, decay_log):
    model = fine_rows.shape[1]
    fine_count = fine_rows.shape[0]
    heads, rows_coarse = decay_log.shape
    width = heads * HD
    place = jnp.reshape(lax.axis_index("mp"), (1,)).astype(jnp.int32)
    core = jnp.reshape(lax.axis_index("seq") % 2, (1,)).astype(jnp.int32)

    before = passed_along(fine_rows[fine_count - 16 :], ("seq", "mp"), 1)
    p0, p1 = pool(fine_rows, before)
    x1 = swapped(p1, "mp", 1)
    y1 = swapped(p1, "mp", 2)
    x0 = swapped(p0, "mp", 1)
    y0 = swapped(p0, "mp", 2)
    cum_rows, cum_columns, total = decay_sums(decay_log, p0)
    parts = 2
    w_q, w_k, w_v, w_g = weights = list(zip(*[prepare(w_inputs, part, parts, total) for part in range(parts)]))
    d1 = swapped(y1, "mp", 1)

    types = [BF, BF, BF, F32]
    first = project([p0, p1], weights, types, y1)
    x0 = held_back(x0, first[0])
    d0 = swapped(x0, "mp", 2)
    second = project([x1, y1], weights, types)
    third = project([x0, y0], weights, types)
    known, left = in_vmem(*known_state(place, [first, second, third], cum_columns, width))
    k_last, v_last, state = last_keys_and_state([d0, d1], w_k, w_v, known, left, total, width)
    k_last, v_last = in_vmem(k_last, v_last)
    other = swapped(state, "seq", 1)
    q_last, g_last = project([d0, d1], [w_q, w_g], [BF, F32])
    chip_state = state_of_chip(core, state, other, total)
    chip_states = [passed_along(chip_state, "seq", 2 * d) for d in range(1, lax.axis_size("seq") // 2)]
    groups, w_kept, attended = local_attention(
        place, [first, second, third, [q_last, k_last, v_last]], pltpu.with_memory_space_constraint(w_out, pltpu.HBM), cum_columns, cum_rows, width
    )
    own, second, third, last = [(*group, gate) for group, gate in zip(groups, (first[3], second[3], third[3], g_last))]
    entering = entering_chip(chip_states, attended)
    incoming = entering_shard(core, entering, swapped(entering, "seq", 1), other)

    gain = head_gain[None]
    terms = lambda parts: output_terms(parts, gain, incoming, w_kept)
    far_a, far_b = terms([(*last, 0), (*last, 1)])
    got_a = swapped(far_a, "mp", 1)
    got_b = swapped(far_b, "mp", 2)
    x_a, x_b = terms([(*third, 0), (*second, 0)])
    from_x_a = swapped(x_a, "mp", 1)
    y_a, y_b = terms([(*third, 1), (*second, 1)])
    from_y_b = swapped(y_b, "mp", 2)
    own_a, own_b = terms([(*own, 0), (*own, 1)])
    half = model // 2
    widths = (half * 11 // 16, half * 5 // 16)
    from_x_b = [swapped(part, "mp", 1) for part in merged(x_b, got_b, widths, own_a)]
    from_y_a = [swapped(part, "mp", 2) for part in merged(y_a, got_a, widths, own_a)]
    out = None
    for n in range(len(widths)):
        at = sum(widths[:n])
        out = add_coarse(
            fine_rows,
            [
                (at, [(own_a, at), (from_x_a, at), (from_y_a[n], 0)]),
                (half + at, [(own_b, at), (from_y_b, at), (from_x_b[n], 0)]),
            ],
            widths[n],
            out,
        )
    return out


def body(fine_rows, w_inputs, w_out, head_gain, decay_log):
    model_width = fine_rows.shape[1]
    head_dim = D // ATTENDER_NUMBER
    local_heads = decay_log.shape[0]
    local_width = local_heads * head_dim
    rows_coarse = decay_log.shape[1]
    blocks = rows_coarse // CH
    fine_count = fine_rows.shape[0]
    tail_rows = fine_rows[fine_count - (SF - 1) :]
    before = passed_along(tail_rows, ("seq", "mp"), 1)
    widened = jnp.concatenate([before, fine_rows[: fine_count - (SF - 1)]], axis=0).astype(
        jnp.float32
    )
    pooled = jnp.mean(widened.reshape(-1, SF, model_width), axis=1).astype(jnp.bfloat16)
    weights_flat = w_inputs.reshape(model_width, 4 * local_width)
    projected = jnp.dot(
        lax.all_gather(pooled, "mp", axis=0, tiled=True),
        weights_flat,
        preferred_element_type=jnp.float32,
    )
    queries = (
        projected[:, :local_width].astype(jnp.bfloat16).reshape(blocks, CH, local_heads, head_dim)
    )
    key_rows = (
        projected[:, local_width : 2 * local_width]
        .astype(jnp.bfloat16)
        .reshape(blocks, CH, local_heads, head_dim)
    )
    values = (
        projected[:, 2 * local_width : 3 * local_width]
        .astype(jnp.bfloat16)
        .reshape(blocks, CH, local_heads, head_dim)
    )
    gate_values = projected[:, 3 * local_width :]
    cumulative = jnp.cumsum(decay_log.reshape(local_heads, blocks, CH), axis=2)
    gaps = cumulative[:, :, :, None] - cumulative[:, :, None, :]
    causal = jnp.arange(CH)[:, None] >= jnp.arange(CH)[None, :]
    weight = jnp.where(causal, jnp.exp(jnp.minimum(gaps, 0.0)), 0.0)
    scores = jnp.einsum("cthd,cshd->hcts", queries, key_rows, preferred_element_type=jnp.float32)
    scores = (scores * weight).astype(jnp.bfloat16)
    within = jnp.einsum("hcts,cshd->cthd", scores, values, preferred_element_type=jnp.float32)
    remaining = jnp.exp(cumulative[:, :, -1:] - cumulative)
    decayed_keys = (
        key_rows.astype(jnp.float32) * jnp.transpose(remaining, (1, 2, 0))[..., None]
    ).astype(jnp.bfloat16)
    block_states = jnp.einsum(
        "cshd,cshe->chde", decayed_keys, values, preferred_element_type=jnp.float32
    )
    block_decay = cumulative[:, :, -1]
    prefix_states = []
    prefix_decay = []
    running = jnp.zeros((local_heads, head_dim, head_dim), jnp.float32)
    decay_total = jnp.zeros((local_heads,), jnp.float32)
    for block_index in range(blocks):
        prefix_states.append(running)
        prefix_decay.append(decay_total)
        running = (
            jnp.exp(block_decay[:, block_index])[:, None, None] * running
            + block_states[block_index]
        )
        decay_total = decay_total + block_decay[:, block_index]
    shard_totals = lax.all_gather(decay_total[None, :], "seq", axis=0, tiled=True)
    my_rank = lax.axis_index("seq")
    running_ends = jnp.cumsum(shard_totals, axis=0)
    before_mine = lax.dynamic_slice_in_dim(running_ends - shard_totals, my_rank, 1, 0)
    shard_states = lax.all_gather(
        running[None].astype(jnp.bfloat16), "seq", axis=0, tiled=True
    ).astype(jnp.float32)
    row_count = shard_states.shape[0]
    span_sums = before_mine - running_ends
    device_rank = jnp.arange(row_count, dtype=jnp.int32)
    factor = jnp.where((device_rank < my_rank)[:, None], jnp.exp(jnp.minimum(span_sums, 0.0)), 0.0)
    incoming = jnp.zeros_like(running) + jnp.sum(factor[:, :, None, None] * shard_states, axis=0)
    entering = jnp.stack(
        [
            jnp.exp(prefix_decay[block_index])[:, None, None] * incoming
            + prefix_states[block_index]
            for block_index in range(blocks)
        ]
    )
    carried = jnp.einsum(
        "cthd,chde->cthe",
        queries,
        entering.astype(jnp.bfloat16),
        preferred_element_type=jnp.float32,
    )
    carried = carried * jnp.transpose(jnp.exp(cumulative), (1, 2, 0))[..., None]
    attended = (within + carried).reshape(rows_coarse, local_heads, head_dim)
    square_mean = jnp.mean(attended * attended, axis=2, keepdims=True)
    normed = (attended * lax.rsqrt(square_mean + EPSILON)).reshape(rows_coarse, local_width)
    gated_rows = (normed * head_gain * jax.nn.silu(gate_values)).astype(jnp.bfloat16)
    coarse = lax.psum_scatter(
        jnp.dot(gated_rows, w_out, preferred_element_type=jnp.float32).astype(jnp.bfloat16),
        "mp",
        scatter_dimension=0,
        tiled=True,
    ).astype(jnp.float32)
    upsampled = jnp.repeat(coarse, SF, axis=0)
    return (fine_rows.astype(jnp.float32) + upsampled).astype(jnp.bfloat16)


def solution(mesh):
    square = mesh.shape["mp"] == 4 and mesh.shape["seq"] % 2 == 0 and mesh.shape["seq"] > 2
    return jax.shard_map(
        body_square if square else body,
        mesh=mesh,
        in_specs=(
            P(("seq", "mp"), None),
            P(None, None, "mp"),
            P("mp", None),
            P("mp"),
            P("mp", "seq"),
        ),
        out_specs=P(("seq", "mp"), None),
        check_vma=False,
    )
```
